256 devices in a mesh: member: 16 (over y, x), band: 16 (over z, core).
Axes of the slice: x: 4, y: 4, z: 8, core: 2. Of those that a mesh axis runs over, the one named last changes fastest.
Arguments:
- ensemble: bfloat16 [16, 64, 80, 1440], P('member', 'band'), may hold values from -6 to 6
- mix_weight: bfloat16 [3, 80, 80], replicated, may hold values from -0.625 to 0.625
- analysis: bfloat16 [64, 80, 1440], P('band', 'member'), may hold values from -4 to 4
- station_weight: bfloat16 [256, 32, 4, 128], P('band'), may hold values from -0.25 to 0.25
- station_obs: bfloat16 [256, 32, 80], P('band'), may hold values from -4 to 4
- block_band: int32 [256, 1], replicated, may hold values from 0 to 15; in each aligned block of 16 rows (0 to 15, 16 to 31, ...) at most 2 rows name the same one
- block_start: int32 [256], replicated, may hold values from 0 to 1312
Outputs:
- grid_score: float32 [64, 80, 1440], P('band', 'member')
- station_score: float32 [256, 32, 80], P('band')
- state_grad: bfloat16 [16, 64, 80, 1440], P('member', 'band')
The draws below stay inside these ranges and needn't reach their ends.
Inputs may be any that keep to these rules, and one draw needn't show every extreme that they name: `block_band`: blocks 16 b to 16 (b + 1) - 1 are stored with band b. Within each such group no band index appears more than 2 times, and some band index appears exactly 2 times.
All inputs are finite; a program needn't handle non-finite values.
Results may differ from the reference program's by a relative error of at most 0.012.
Values may be sent and summed in bfloat16 or wider, within the bound.
A program may use at most 128 MiB of HBM per device.

```python
import math
import jax
import jax.numpy as jnp
import numpy as np
from jax import lax

F = 80
LON = 1440
LAT_DEV = 4
LAYERS = 3
SB = 32
WIN = 128
BLK_DEV = 16
CAP = 2
NLAT = 64
MEMBERS = 16
NBLK = 256
N_BAND = 16


def with_ends(drawn, key, smallest, largest):
    index_at = [jax.random.randint(jax.random.fold_in(key, axis), (), 0, length) for axis, length in enumerate(drawn.shape)]
    longest = drawn.shape.index(max(drawn.shape))
    next_to = index_at[:longest] + [(index_at[longest] + 1) % drawn.shape[longest]] + index_at[longest + 1:]
    return drawn.at[tuple(index_at)].set(smallest).at[tuple(next_to)].set(largest)


def block_scale(own_key, extent, pieces, low, high):
    factor_of, own = 1.0, jax.random.fold_in(own_key, 6)
    for axis_at, parts in pieces:
        heights = jnp.exp(jax.random.uniform(jax.random.fold_in(own, axis_at), (parts,), jnp.float32, low / len(pieces), high / len(pieces)))
        factor_of = factor_of * jnp.repeat(heights, extent[axis_at] // parts).reshape([-1 if axis == axis_at else 1 for axis in range(len(extent))])
    return factor_of


def deal_out(rng, own, number, rows, count, top, limit, skew):
    sequence = jax.random.permutation(rng, count)
    packed, common = shares(count, rows * top, limit, skew, True), shares(count, rows * top, limit, skew, False)
    places = jnp.arange(count)

    def named(sizes, offset_by):
        used = int((sizes > 0).sum())
        fixed = max(1, used // 4)
        shifted = fixed + (places - fixed + offset_by * (used - fixed)) % max(1, count - fixed)
        return jnp.zeros((count,), jnp.int32).at[sequence[jnp.where(places < fixed, places, shifted)]].set(jnp.asarray(sizes, jnp.int32))

    sizes = jnp.where(number % 4 == 0, named(packed, number // 4), named(common, number - number // 4 - 1))
    mixed = jax.random.permutation(jax.random.fold_in(own, 3), count)
    giver, sink = mixed[0:count // 2 * 2:2], mixed[1:count // 2 * 2:2]
    room = jnp.minimum(sizes[giver] - 1, limit - sizes[sink]) // 2
    room = jnp.where((giver == sequence[0]) | (sink == sequence[0]) | (sizes[sink] == 0), 0, jnp.maximum(room, 0))
    shifted = jax.random.randint(jax.random.fold_in(own, 4), (count // 2,), 0, 1 << 20) % (room + 1)
    sizes = sizes.at[giver].add(-shifted).at[sink].add(shifted)
    items = jnp.searchsorted(jnp.cumsum(sizes), jnp.arange(rows * top), side="right").astype(jnp.int32)
    table = items.reshape(top, rows).T
    table = table[jax.random.permutation(jax.random.fold_in(own, 1), rows)]
    offset_by = jax.random.randint(jax.random.fold_in(own, 2), (rows, 1), 0, top)
    return jnp.take_along_axis(table, (jnp.arange(top)[None, :] + offset_by) % top, axis=1)


def shares(count, total, most, skew, full):
    portions = [(1 << 20) // math.isqrt(standing ** skew) + 1 for standing in range(1, count + 1)]
    largest = most if full else min(most, max(-(-total // count), total * portions[0] // sum(portions)))
    least = 1 if total - largest >= count - 1 else 0
    counts, spare = [largest] + [least] * (count - 1), total - largest - least * (count - 1)
    while spare > 0:
        movable = [i for i in range(1, count) if counts[i] < largest] or [i for i in range(1, count) if counts[i] < most]
        whole, remaining = sum([portions[i] for i in movable]), spare
        for i in movable:
            addition = min(most - counts[i], max(1, remaining * portions[i] // whole), spare)
            counts[i] = counts[i] + addition
            spare = spare - addition
    return np.array(counts)


def centred(key, shape, scale, bound, pieces=(), held_as=jnp.bfloat16):
    array = jax.random.normal(key, shape, jnp.float32) * scale
    if len(pieces) > 0:
        array = block_scale(key, shape, pieces, -0.22, 0.18) * array
    return jnp.clip(array, min=-bound, max=bound).astype(held_as)


def setup_inputs(seed: int = 0) -> dict:
    arg_keys = jax.random.split(jax.random.key(seed), 8)
    ensemble = centred(arg_keys[0], (MEMBERS, NLAT, F, LON), 1.0, 6.0, ((0, 16), (1, 16)))
    mix_weight = centred(arg_keys[1], (LAYERS, F, F), F ** -0.5, 0.625)
    analysis = centred(arg_keys[2], (NLAT, F, LON), 0.5, 4.0, ((0, 16), (1, 16)))
    station_weight = centred(arg_keys[3], (NBLK, SB, LAT_DEV, WIN), (LAT_DEV * WIN) ** -0.5, 0.25, ((0, 16),))
    station_obs = centred(arg_keys[4], (NBLK, SB, F), 0.5, 4.0, ((0, 16),))
    block_band_keys = jax.random.split(jax.random.fold_in(arg_keys[5], 1), NBLK // BLK_DEV)
    block_band_turns = jax.random.permutation(jax.random.fold_in(arg_keys[5], 3), NBLK // BLK_DEV)
    block_band = jax.vmap(lambda own, number: deal_out(jax.random.fold_in(arg_keys[5], 2), own, number, BLK_DEV, N_BAND, 1, CAP, 2))(block_band_keys, block_band_turns).reshape((NBLK, 1))
    block_start = with_ends(jax.random.randint(arg_keys[6], (NBLK,), 0, LON - WIN + 1), jax.random.fold_in(arg_keys[6], 1), 0, LON - WIN).astype(jnp.int32)
    return {"ensemble": ensemble, "mix_weight": mix_weight, "analysis": analysis, "station_weight": station_weight, "station_obs": station_obs, "block_band": block_band, "block_start": block_start}


DIFFUSION = 4.0

def kernel_value(spread):
    return jnp.sqrt(spread * spread + 1.0) - 1.0

def kernel_slope(spread):
    return spread / jnp.sqrt(spread * spread + 1.0)

def metric_rows(global_rows, total_rows):
    latitude = math.pi * ((global_rows.astype(jnp.float32) + 0.5) / total_rows - 0.5)
    cosine = jnp.cos(latitude)
    return 1.0 / (cosine * cosine + 0.1)

def inverse_table(points):
    centre = 1.0 + 2.0 * DIFFUSION
    decay_root = (centre - math.sqrt(centre * centre - 4.0 * DIFFUSION * DIFFUSION)) / (2.0 * DIFFUSION)
    log_root = math.log(decay_root)
    factor = 1.0 / (DIFFUSION * (1.0 / decay_root - decay_root) * (1.0 - decay_root ** points))
    column = lax.broadcasted_iota(jnp.int32, (points, points), 0)
    across = lax.broadcasted_iota(jnp.int32, (points, points), 1)
    offset = jnp.abs(column - across)
    nearest = jnp.minimum(offset, points - offset).astype(jnp.float32)
    values = (jnp.exp(nearest * log_root) + jnp.exp((points - nearest) * log_root)) * factor
    return values.astype(jnp.bfloat16)

def pair_sums(samples):

    def pair_step(running, other_member):
        spread = samples - other_member[None]
        return ((running[0] + kernel_value(spread), running[1] + kernel_slope(spread)), None)
    zero_start = jnp.zeros(samples.shape, jnp.float32)
    result, _ = lax.scan(pair_step, (zero_start, zero_start), samples)
    return result

def reference(ensemble, mix_weight, analysis, station_weight, station_obs, block_band, block_start):
    current = ensemble
    metric = metric_rows(jnp.arange(NLAT, dtype=jnp.int32), NLAT)[None, :, None, None]
    for layer_pos in range(LAYERS):
        padded = jnp.pad(current, ((0, 0), (1, 1), (0, 0), (0, 0)))
        middle = current.astype(jnp.float32)
        north = padded[:, 2:].astype(jnp.float32)
        south = padded[:, :-2].astype(jnp.float32)
        eastward = jnp.roll(middle, -1, axis=3)
        westward = jnp.roll(middle, 1, axis=3)
        laplace = (eastward + westward - 2.0 * middle) * metric + (north + south - 2.0 * middle)
        scaled = (laplace / (2.0 + 2.0 * metric)).astype(jnp.bfloat16)
        mixed = jnp.einsum('fg,mrgl->mrfl', mix_weight[layer_pos].astype(jnp.float32), scaled.astype(jnp.float32))
        current = (middle + jnp.tanh(mixed)).astype(jnp.bfloat16)
    inverse = inverse_table(LON)
    diffused = jnp.dot(current.reshape(-1, LON), inverse, preferred_element_type=jnp.float32)
    diffused = diffused.reshape(current.shape).astype(jnp.bfloat16)
    values = diffused.astype(jnp.float32)
    pair_value, pair_slope = pair_sums(values)
    error_field = values - analysis.astype(jnp.float32)[None]
    pair_scale = 1.0 / (2.0 * MEMBERS * (MEMBERS - 1))
    grid_score = lax.optimization_barrier(jnp.sum(kernel_value(error_field) / MEMBERS - pair_value * pair_scale, axis=0))
    grid_grad = kernel_slope(error_field) - pair_slope / (MEMBERS - 1)
    band_list = block_band[:, 0].astype(jnp.int32)
    anchor = jnp.zeros((), jnp.int32)

    def estimate_block(inputs):
        band_id, first_lon, weight = inputs
        block_rows = lax.dynamic_slice(diffused, (anchor, (band_id * LAT_DEV).astype(jnp.int32), anchor, first_lon.astype(jnp.int32)), (MEMBERS, LAT_DEV, F, WIN))
        return jnp.einsum('srw,mrfw->msf', weight.astype(jnp.float32), block_rows.astype(jnp.float32))
    estimates = lax.map(estimate_block, (band_list, block_start, station_weight))
    ensemble_est = jnp.transpose(estimates, (1, 0, 2, 3))
    station_value, station_pull = pair_sums(ensemble_est)
    station_miss = ensemble_est - station_obs.astype(jnp.float32)[None]
    station_score = lax.optimization_barrier(jnp.sum(kernel_value(station_miss) / MEMBERS - station_value * pair_scale, axis=0))
    station_slopes = (kernel_slope(station_miss) - station_pull / (MEMBERS - 1)).astype(jnp.bfloat16)

    def add_block(running, inputs):
        band_id, first_lon, weight, slope_block = inputs
        contribution = jnp.einsum('srw,msf->mrfw', weight.astype(jnp.float32), slope_block.astype(jnp.float32))
        corner = (anchor, (band_id * LAT_DEV).astype(jnp.int32), anchor, first_lon.astype(jnp.int32))
        existing = lax.dynamic_slice(running, corner, contribution.shape)
        return (lax.dynamic_update_slice(running, existing + contribution, corner), None)
    station_grad, _ = lax.scan(add_block, jnp.zeros(diffused.shape, jnp.float32), (band_list, block_start, station_weight, jnp.transpose(station_slopes, (1, 0, 2, 3))))
    total_grad = (grid_grad + station_grad).astype(jnp.bfloat16)
    state_grad = jnp.dot(total_grad.reshape(-1, LON), inverse.T, preferred_element_type=jnp.float32)
    state_grad = state_grad.reshape(diffused.shape).astype(jnp.bfloat16)
    return (grid_score, station_score, state_grad)
```

```python
import math

import jax
import jax.numpy as jnp
import numpy as np
from jax import lax
from jax.experimental import pallas as pl
from jax.experimental.pallas import tpu as pltpu
from jax.sharding import PartitionSpec as P

CAP = 2
DIFFUSION = 4.0

ROWS = 4
HALO = 3
EXT = ROWS + 2 * HALO
FIELDS = 80
LON = 1440
LANES = 1536
QUARTER = LANES // 4
MSG = LANES + QUARTER
MEMBERS = 16
BANDS = 16
TOTAL_ROWS = 64
LAYERS = 3
SLOTS = BANDS * CAP
STATIONS = 32
POINTS = SLOTS * STATIONS
PAIRS = MEMBERS * (MEMBERS - 1) // 2
MIB = 1 << 20

BF = jnp.bfloat16
F32 = jnp.float32


def inverse_table():
    centre = 1.0 + 2.0 * DIFFUSION
    root = (centre - math.sqrt(centre * centre - 4.0 * DIFFUSION * DIFFUSION)) / (2.0 * DIFFUSION)
    factor = 1.0 / (DIFFUSION * (1.0 / root - root) * (1.0 - root**LON))
    offset = np.abs(np.arange(LON)[:, None] - np.arange(LON)[None, :])
    nearest = np.minimum(offset, LON - offset).astype(np.float64)
    values = (np.exp(nearest * math.log(root)) + np.exp((LON - nearest) * math.log(root))) * factor
    table = np.zeros((LANES, LANES), np.float32)
    table[:LON, :LON] = values
    return table.astype(BF)


def row_factors():
    rows = np.arange(-HALO, TOTAL_ROWS + HALO)
    cosine = np.cos(math.pi * ((rows + 0.5) / TOTAL_ROWS - 0.5))
    metric = 1.0 / (cosine * cosine + 0.1)
    inside = (rows >= 0) & (rows < TOTAL_ROWS)
    return np.stack([metric / (2 + 2 * metric), 1 / (2 + 2 * metric), inside], axis=1).astype(np.float32)


def hot(condition):
    return jnp.where(condition, 1.0, 0.0).astype(BF)


def iota(shape, dim):
    return lax.broadcasted_iota(jnp.int32, shape, dim)


def grid_to_message(transposed):
    shape = (320, 256) if transposed else (256, 320)
    row, col = iota(shape, int(transposed)), iota(shape, 1 - int(transposed))
    group, place = row >> 4, row & 15
    main = hot(col == (place >> 2) * FIELDS + group * 5 + (place & 3))
    fifth = (col == (place & 3) * FIELDS + group * 5 + 4)
    return main, [hot(fifth & ((place >> 2) == q)) for q in range(4)]


def message_to_station(transposed):
    shape = (256, 512) if transposed else (512, 256)
    row, col = iota(shape, int(transposed)), iota(shape, 1 - int(transposed))
    r, member, f = row >> 7, (row >> 3) & 15, row & 7
    same = member == (col >> 4)
    place = col & 15
    main = hot(same & (f < 4) & (place == r * 4 + f))
    return main, [hot(same & (f == 4) & (place == q * 4 + r)) for q in range(4)]


def dot(a, b):
    return jnp.dot(a, b, preferred_element_type=F32)


def dot_t(a, b):
    return lax.dot_general(a, b, (((1,), (1,)), ((), ())), preferred_element_type=F32)


def stencil_row(u, nxt, scaled, weight, row, east_west, north_south, inside):
    tiles = LANES // 128
    lane = iota((FIELDS, 128), 1)

    def tile(at, t):
        return u[at, :, t * 128 : (t + 1) * 128].astype(F32)

    first, last = tile(row, 0), tile(row, tiles - 1)
    wrapped = jnp.where(lane == LON % 128, pltpu.roll(first, LON % 128, 1), last)
    before = pltpu.roll(last, 129 - LON % 128, 1)
    here = first
    for t in range(tiles):
        after = wrapped if t == tiles - 2 else (tile(row, t + 1) if t < tiles - 1 else here)
        east = jnp.where(lane == 127, pltpu.roll(after, 127, 1), pltpu.roll(here, 127, 1))
        moved = pltpu.roll(here, 1, 1)
        west = jnp.where(lane == 0, before, moved)
        sides = tile(row - 1, t) + tile(row + 1, t)
        value = (east + west) * east_west + sides * north_south - here
        scaled[:, t * 128 : (t + 1) * 128] = value.astype(BF)
        before, here = moved, after
    for t in range(0, LANES, 256):
        mixed = dot(weight, scaled[:, t : t + 256])
        fresh = u[row, :, t : t + 256].astype(F32) + jnp.tanh(mixed)
        nxt[row, :, t : t + 256] = (fresh * inside).astype(BF)


def diffuse_to_message(state, inverse_ref, message_ref):
    main, fifth = grid_to_message(False)
    folded = jnp.zeros((256, QUARTER), F32)
    rows = state[HALO : HALO + ROWS].reshape(ROWS * FIELDS, LANES)
    for q in range(4):
        at = slice(q * QUARTER, (q + 1) * QUARTER)
        piece = dot(rows, inverse_ref[:, at]).astype(BF)
        message_ref[:, :, at] = dot(main, piece).astype(BF).reshape(MEMBERS, 16, QUARTER)
        folded += dot(fifth[q], piece)
    message_ref[:, :, LANES:] = folded.astype(BF).reshape(MEMBERS, 16, QUARTER)


def pair_terms(values, truth):
    slopes = [None] * MEMBERS
    total = None
    for i in range(MEMBERS):
        for j in range(i + 1, MEMBERS):
            spread = values[i] - values[j]
            square = spread * spread + 1.0
            inverse = lax.rsqrt(square)
            slope = spread * inverse
            root = square * inverse
            total = root if total is None else total + root
            slopes[i] = slope if slopes[i] is None else slopes[i] + slope
            slopes[j] = -slope if slopes[j] is None else slopes[j] - slope
    error_total = None
    grads = []
    for m in range(MEMBERS):
        error = values[m] - truth
        square = error * error + 1.0
        inverse = lax.rsqrt(square)
        root = square * inverse
        error_total = root if error_total is None else error_total + root
        grads.append(error * inverse - slopes[m] * (1.0 / (MEMBERS - 1)))
    score = (error_total - MEMBERS) * (1.0 / MEMBERS) - (total - PAIRS) * (1.0 / (MEMBERS * (MEMBERS - 1)))
    return score, grads


def send(src, dst, sems, at, device):
    return pltpu.make_async_remote_copy(
        src_ref=src,
        dst_ref=dst,
        send_sem=sems.at[0, at],
        recv_sem=sems.at[1, at],
        device_id=device,
        device_id_type=pl.DeviceIdType.MESH,
    )


def member_at(member, step, sign):
    x = (member + sign * (step & 3)) & 3
    y = ((member >> 2) + sign * (step >> 2)) & 3
    return y * 4 + x


def band_at(band, step, sign):
    return (band + sign * step) & (BANDS - 1)


def exchange(source, target, sems, me, at, axis):
    @pl.loop(1, 16)
    def _(step):
        peer = at(me, step, 1)
        send(source(peer), target(me), sems, step, {axis: peer}).start()


def wait_received(source, target, sems, me, at, axis):
    @pl.loop(1, 16)
    def _(step):
        peer = at(me, step, -1)
        send(source(peer), target(peer), sems, step, {axis: peer}).wait_recv()


def wait_sent(source, target, sems, me, at, axis):
    @pl.loop(1, 16)
    def _(step):
        peer = at(me, step, 1)
        send(source(peer), target(me), sems, step, {axis: peer}).wait_send()


def outgoing_blocks(slot_ref, share_ref, obs_ref, zout):
    lane = iota((1, 128), 1)
    slot_row = jnp.zeros((1, 128), jnp.int32)
    for k in range(16):
        slot_row = jnp.where((lane >> 3) == k, slot_ref[k], slot_row)
    row, col = iota((256, 128), 0), iota((256, 128), 1)
    pick = hot(((row >> 3) == slot_row) & ((row & 7) == (col & 7)))
    zout[:, 0:16, :] = dot(pick, share_ref[...]).astype(BF).reshape(BANDS, 16, 128)
    group = iota((8, 128), 1) >> 5
    for t in range(SLOTS // 4):
        tile = jnp.zeros((8, 128), F32)
        for k in range(16):
            tile = jnp.where(group + 4 * t == slot_ref[k], obs_ref[k], tile)
        for odd in range(2):
            piece = pltpu.roll(tile, 64, 1) if odd else tile
            zout[2 * t + odd, 16:32, :] = jnp.concatenate([piece, jnp.zeros((8, 128), F32)], axis=0).astype(BF)


def spread_out_weights(start_ref, weights, spread_weight):
    lane = iota((STATIONS, 128), 1)

    @pl.loop(0, BANDS)
    def _(home):
        blocks = [weights[r * 4 : r * 4 + 4, home].astype(F32) for r in range(ROWS)]
        for cap in range(CAP):
            start = start_ref[home * CAP + cap]
            shift = start & 127
            at = pl.ds(home * 64 + cap * STATIONS, STATIONS)
            moved = [
                pltpu.roll(block[:, cap * 8 : cap * 8 + 8, :].reshape(STATIONS, 128), shift, 1)
                for block in blocks
            ]
            for t in range(LANES // 128):
                place = lane + t * 128 - start
                inside = (place >= 0) & (place < 128)
                for r in range(ROWS):
                    spread_weight[r, at, t * 128 : (t + 1) * 128] = jnp.where(inside, moved[r], 0.0).astype(BF)


def fold_truth(truth_ref, truth):
    truth[...] = jnp.zeros((16, MSG), F32)
    for r in range(ROWS):
        row = truth_ref[r].astype(F32)
        truth[4 * r : 4 * r + 4, :LON] = row[0:4]
        for q in range(4):
            width = min(QUARTER, LON - q * QUARTER)
            truth[4 * q + r : 4 * q + r + 1, LANES : LANES + width] = row[4:5, q * QUARTER : q * QUARTER + width]


def join_obs(zin, obs):
    lane = iota((8, 128), 1)
    for t in range(POINTS // 128):
        low = zin[2 * t, 16:32, :].astype(F32)[0:8]
        high = zin[2 * t + 1, 16:32, :].astype(F32)[0:8]
        obs[:, t * 128 : (t + 1) * 128] = jnp.where(lane < 64, low, pltpu.roll(high, 64, 1))


def station_part(received, rows, est, slopes, spread_weight, spread, obs, station_out):
    main, fifth = message_to_station(False)
    for q in range(4):
        at = slice(q * QUARTER, (q + 1) * QUARTER)
        rows[:, at] = (
            dot(main, received[:, :, at].reshape(256, QUARTER))
            + dot(fifth[q], received[:, :, LANES:].reshape(256, QUARTER))
        ).astype(BF)

    @pl.loop(0, POINTS // 256)
    def _(n):
        at = pl.ds(pl.multiple_of(n * 256, 256), 256)
        total = jnp.zeros((128, 256), F32)
        for r in range(ROWS):
            total += dot_t(rows[r * 128 : (r + 1) * 128, :], spread_weight[r, at, :])
        est[:, at] = total

    lane = iota((8, 128), 1)

    @pl.loop(0, POINTS // 128)
    def _(n):
        at = pl.ds(pl.multiple_of(n * 128, 128), 128)
        members = [est[m * 8 : (m + 1) * 8, at] for m in range(MEMBERS)]
        total, grads = pair_terms(members, obs[:, at])
        other = pltpu.roll(total, 64, 1)
        station_out[2 * n] = jnp.where(lane < 64, total, other)
        station_out[2 * n + 1] = jnp.where(lane < 64, other, total)
        for m in range(MEMBERS):
            est[m * 8 : (m + 1) * 8, at] = grads[m]

    slopes[...] = est[...].astype(BF)


def spread_slopes(slopes, spread_weight, spread):
    for r in range(ROWS):
        @pl.loop(0, LANES // 256)
        def _(n):
            at = pl.ds(pl.multiple_of(n * 256, 256), 256)
            spread[r * 128 : (r + 1) * 128, at] = dot(slopes[...], spread_weight[r, :, at]).astype(BF)


def grid_part(received, values, truth, score):
    values[...] = received[...].astype(F32)

    @pl.loop(0, MSG // 128)
    def _(n):
        at = pl.ds(pl.multiple_of(n * 128, 128), 128)
        for half in range(2):
            part = slice(half * 8, half * 8 + 8)
            members = [values[m, part, at] for m in range(MEMBERS)]
            total, grads = pair_terms(members, truth[part, at])
            score[part, at] = total
            for m in range(MEMBERS):
                values[m, part, at] = grads[m]


def total_gradient(values, spread, grad):
    back, back_fifth = message_to_station(True)
    folded = jnp.zeros((256, QUARTER), F32)
    for q in range(4):
        at = slice(q * QUARTER, (q + 1) * QUARTER)
        total = values[:, :, at].reshape(256, QUARTER) + dot(back, spread[:, at])
        grad[:, :, at] = total.astype(BF).reshape(MEMBERS, 16, QUARTER)
        folded += dot(back_fifth[q], spread[:, at])
    total = values[:, :, LANES:].reshape(256, QUARTER) + folded
    grad[:, :, LANES:] = total.astype(BF).reshape(MEMBERS, 16, QUARTER)


def unfold_score(score, score_ref):
    for r in range(ROWS):
        score_ref[r, 0:4, :] = score[4 * r : 4 * r + 4, :LON]
        for q in range(4):
            width = min(QUARTER, LON - q * QUARTER)
            score_ref[r, 4:5, q * QUARTER : q * QUARTER + width] = score[
                4 * q + r : 4 * q + r + 1, LANES : LANES + width
            ]


def own_station_scores(slot_ref, station_in, own):
    group = iota((8, 128), 1) >> 5
    even = (group & 1) == 0
    pieces = []
    for b in range(BANDS):
        here = station_in[b]
        moved = pltpu.roll(here, 32, 1)
        pieces.append(jnp.where(even, here, moved))
        pieces.append(jnp.where(even, moved, here))
    for t in range(4):
        slot = jnp.zeros((8, 128), jnp.int32)
        for g in range(4):
            slot = jnp.where(group == g, slot_ref[4 * t + g], slot)
        tile = jnp.zeros((8, 128), F32)
        for at in range(SLOTS):
            tile = jnp.where(slot == at, pieces[at], tile)
        own[:, t * 128 : (t + 1) * 128] = tile


def all_station_scores(gathered, station_ref):
    row, col = iota((128, FIELDS), 0), iota((128, FIELDS), 1)
    pick = hot(((row & 7) < 5) & ((row >> 3) * 5 + (row & 7) == col))
    whole = gathered[...].reshape(128, 512)
    high = whole.astype(BF)
    low = (whole - high.astype(F32)).astype(BF)
    dims = (((0,), (0,)), ((), ()))
    joined = lax.dot_general(high, pick, dims, preferred_element_type=F32)
    joined += lax.dot_general(low, pick, dims, preferred_element_type=F32)
    station_ref[...] = joined.reshape(16, STATIONS, FIELDS)


def state_part(returned, inverse, total, out_ref):
    main, fifth = grid_to_message(True)
    for q in range(4):
        at = slice(q * QUARTER, (q + 1) * QUARTER)
        total[:, at] = (
            dot(main, returned[:, :, at].reshape(256, QUARTER))
            + dot(fifth[q], returned[:, :, LANES:].reshape(256, QUARTER))
        ).astype(BF)
    for q in range(4):
        width = min(QUARTER, LON - q * QUARTER)
        at = slice(q * QUARTER, q * QUARTER + width)
        out_ref[0, :, :, at] = dot(total[...], inverse[:, at]).astype(BF).reshape(ROWS, FIELDS, width)


def kernel(
    start_ref, slot_ref, factor_ref, state_ref, mix_ref, share_ref, obs_ref, truth_ref, inverse_ref,
    score_ref, station_ref, out_ref,
    layers, scaled, inverse, zout, zin, weights, spread_weight, message, received, grad, returned,
    rows, est, slopes, values, spread, truth, obs, score, station_out, station_in, own, gathered, total,
    inverse_sem, halo_sem, z_sem, weight_sem, message_sem, station_sem, own_sem, grad_sem,
):
    band = lax.axis_index("band")
    member = lax.axis_index("member")
    fetch = pltpu.make_async_copy(inverse_ref, inverse, inverse_sem)
    fetch.start()

    barrier = pltpu.get_barrier_semaphore()
    u = layers.at[0]
    u[HALO : HALO + ROWS, :, LON - 32 :] = jnp.zeros((ROWS, FIELDS, LANES - LON + 32), BF)
    u[HALO : HALO + ROWS, :, :LON] = state_ref[0]

    @pl.when(band == 0)
    def _():
        u[0:HALO] = jnp.zeros((HALO, FIELDS, LANES), BF)

    @pl.when(band == BANDS - 1)
    def _():
        u[HALO + ROWS :] = jnp.zeros((HALO, FIELDS, LANES), BF)

    @pl.loop(1, 16)
    def _(step):
        for device in ({"member": member_at(member, step, 1)}, {"band": band_at(band, step, 1)}):
            pl.semaphore_signal(barrier, inc=1, device_id=device, device_id_type=pl.DeviceIdType.MESH)

    outgoing_blocks(slot_ref, share_ref, obs_ref, zout)
    pl.semaphore_wait(barrier, 30)

    def to_north(i):
        return send(u.at[HALO + ROWS - 1 - i], u.at[HALO - 1 - i], halo_sem, i, {"band": band_at(band, 1, 1)})

    def to_south(i):
        return send(u.at[HALO + i], u.at[HALO + ROWS + i], halo_sem, HALO + i, {"band": band_at(band, 1, -1)})

    for i in range(HALO):
        pl.when(band < BANDS - 1)(to_north(i).start)
        pl.when(band > 0)(to_south(i).start)

    z_args = (lambda b: zout.at[b], lambda b: zin.at[b], z_sem, band, band_at, "band")
    weight_args = (
        lambda m: zin.at[:, 0:16, :], lambda m: weights.at[m], weight_sem, member, member_at, "member"
    )
    message_args = (lambda m: message.at[m], lambda m: received.at[m], message_sem, member, member_at, "member")
    station_args = (lambda b: station_out.at[b], lambda b: station_in.at[b], station_sem, band, band_at, "band")
    own_args = (lambda m: own, lambda m: gathered.at[m], own_sem, member, member_at, "member")
    grad_args = (lambda m: grad.at[m], lambda m: returned.at[m], grad_sem, member, member_at, "member")

    exchange(*z_args)
    zin[band] = zout[band]

    def run_layer(layer, first, stop):
        @pl.loop(first, stop)
        def _(row):
            factor = band * ROWS + row
            stencil_row(
                layers.at[layer], layers.at[layer + 1], scaled, mix_ref[layer], row,
                factor_ref[factor, 0], factor_ref[factor, 1], factor_ref[factor, 2],
            )

    def run_pair(layer, low, high):
        @pl.loop(0, 2)
        def _(side):
            row = low + side * (high - low)
            factor = band * ROWS + row
            stencil_row(
                layers.at[layer], layers.at[layer + 1], scaled, mix_ref[layer], row,
                factor_ref[factor, 0], factor_ref[factor, 1], factor_ref[factor, 2],
            )

    def wait_halo(i):
        pl.when(band > 0)(to_north(i).wait_recv)
        pl.when(band < BANDS - 1)(to_south(i).wait_recv)

    run_layer(0, 4, 6)
    wait_halo(0)
    run_pair(0, 3, 6)
    wait_received(*z_args)
    exchange(*weight_args)
    weights[member] = zin[:, 0:16, :]
    wait_halo(1)
    run_pair(0, 2, 7)
    run_layer(1, 3, 7)
    wait_halo(2)
    run_pair(0, 1, 8)
    run_pair(1, 2, 7)
    run_layer(2, 3, 7)

    fetch.wait()
    diffuse_to_message(layers.at[LAYERS], inverse, message)
    exchange(*message_args)
    received[member] = message[member]

    fold_truth(truth_ref, truth)
    join_obs(zin, obs)
    wait_received(*weight_args)
    spread_out_weights(start_ref, weights, spread_weight)
    wait_received(*message_args)

    station_part(received, rows, est, slopes, spread_weight, spread, obs, station_out)
    exchange(*station_args)
    station_in[band] = station_out[band]
    spread_slopes(slopes, spread_weight, spread)
    grid_part(received, values, truth, score)
    total_gradient(values, spread, grad)
    exchange(*grad_args)
    returned[member] = grad[member]

    wait_received(*station_args)
    own_station_scores(slot_ref, station_in, own)
    exchange(*own_args)
    gathered[member] = own[...]
    unfold_score(score, score_ref)

    wait_received(*own_args)
    all_station_scores(gathered, station_ref)
    wait_received(*grad_args)
    state_part(returned, inverse, total, out_ref)

    for i in range(HALO):
        pl.when(band < BANDS - 1)(to_north(i).wait_send)
        pl.when(band > 0)(to_south(i).wait_send)
    for args in (z_args, weight_args, message_args, station_args, own_args, grad_args):
        wait_sent(*args)


def slot_tables(block_band, block_start, band_pos):
    band_table = block_band[:, 0].reshape(BANDS, -1)
    start_table = block_start.reshape(BANDS, -1)
    order = jnp.arange(band_table.shape[1], dtype=jnp.int32)
    earlier = (band_table[:, :, None] == band_table[:, None, :]) & (order[:, None] > order[None, :])
    rank_table = jnp.sum(earlier.astype(jnp.int32), axis=2)
    caps = jnp.arange(CAP, dtype=jnp.int32)
    mine = (band_table[:, None, :] == band_pos) & (rank_table[:, None, :] == caps[:, None])
    starts = jnp.sum(jnp.where(mine, start_table[:, None, :], 0), axis=2).reshape(SLOTS)
    slot_table = band_table * CAP + rank_table
    return starts, lax.dynamic_index_in_dim(slot_table, band_pos, 0, keepdims=False)


def shards(ensemble, mix_weight, analysis, station_weight, station_obs, block_band, block_start):
    band_pos = lax.axis_index("band")
    member_pos = lax.axis_index("member")
    starts, slots = slot_tables(block_band, block_start, band_pos)
    share = lax.dynamic_slice(
        station_weight, (0, (member_pos & 3) * 8, member_pos >> 2, 0), (16, 8, 1, 128)
    ).reshape(128, 128)
    obs_share = jnp.transpose(lax.dynamic_slice_in_dim(station_obs, member_pos * 5, 5, 2), (0, 2, 1))
    obs_share = jnp.tile(jnp.pad(obs_share, ((0, 0), (0, 3), (0, 0))), (1, 1, 4)).astype(F32)

    smem = pl.BlockSpec(memory_space=pltpu.SMEM)
    vmem = pl.BlockSpec(memory_space=pltpu.VMEM)
    message = (MEMBERS, 16, MSG)
    sems = pltpu.SemaphoreType.DMA((2, 16))
    return pl.pallas_call(
        kernel,
        out_shape=(
            jax.ShapeDtypeStruct((ROWS, 5, LON), F32),
            jax.ShapeDtypeStruct((16, STATIONS, FIELDS), F32),
            jax.ShapeDtypeStruct((1, ROWS, FIELDS, LON), BF),
        ),
        in_specs=[smem] * 3 + [vmem] * 5 + [pl.BlockSpec(memory_space=pl.ANY)],
        out_specs=(vmem, vmem, vmem),
        scratch_shapes=[
            pltpu.VMEM((LAYERS + 1, EXT, FIELDS, LANES), BF),
            pltpu.VMEM((FIELDS, LANES), BF),
            pltpu.VMEM((LANES, LANES), BF),
            pltpu.VMEM((BANDS, 32, 128), BF),
            pltpu.VMEM((BANDS, 32, 128), BF),
            pltpu.VMEM((MEMBERS, BANDS, 16, 128), BF),
            pltpu.VMEM((ROWS, POINTS, LANES), BF),
            pltpu.VMEM(message, BF),
            pltpu.VMEM(message, BF),
            pltpu.VMEM(message, BF),
            pltpu.VMEM(message, BF),
            pltpu.VMEM((512, LANES), BF),
            pltpu.VMEM((128, POINTS), F32),
            pltpu.VMEM((128, POINTS), BF),
            pltpu.VMEM(message, F32),
            pltpu.VMEM((512, LANES), BF),
            pltpu.VMEM((16, MSG), F32),
            pltpu.VMEM((8, POINTS), F32),
            pltpu.VMEM((16, MSG), F32),
            pltpu.VMEM((BANDS, 8, 128), F32),
            pltpu.VMEM((BANDS, 8, 128), F32),
            pltpu.VMEM((8, 512), F32),
            pltpu.VMEM((MEMBERS, 8, 512), F32),
            pltpu.VMEM((ROWS * FIELDS, LANES), BF),
            pltpu.SemaphoreType.DMA,
            sems, sems, sems, sems, sems, sems, sems,
        ],
        compiler_params=pltpu.CompilerParams(
            vmem_limit_bytes=56 * MIB, collective_id=0, has_side_effects=True
        ),
    )(
        starts, slots, jnp.asarray(row_factors()), ensemble, mix_weight, share, obs_share, analysis,
        jnp.asarray(inverse_table()),
    )


def solution(mesh):
    return jax.shard_map(
        shards,
        mesh=mesh,
        in_specs=(
            P("member", "band", None, None),
            P(),
            P("band", "member", None),
            P("band", None, None, None),
            P("band", None, None),
            P(),
            P(),
        ),
        out_specs=(
            P("band", "member", None),
            P("band", None, None),
            P("member", "band", None, None),
        ),
        check_vma=False,
    )
```

```python
import math

import jax
import jax.numpy as jnp
import numpy as np
from jax import lax
from jax.experimental import pallas as pl
from jax.experimental.pallas import tpu as pltpu
from jax.sharding import PartitionSpec as P

CAP = 2
DIFFUSION = 4.0

ROWS = 4
HALO = 3
EXT = ROWS + 2 * HALO
FIELDS = 80
LON = 1440
LANES = 1536
CHUNKS = 3
CHUNK = LANES // CHUNKS
TILES = CHUNK // 128
PIECE = CHUNK + 128
MEMBERS = 16
BANDS = 16
TOTAL_ROWS = 64
LAYERS = 3
SLOTS = BANDS * CAP
STATIONS = 32
POINTS = SLOTS * STATIONS
PAIRS = MEMBERS * (MEMBERS - 1) // 2
MIB = 1 << 20

BF = jnp.bfloat16
F32 = jnp.float32


def inverse_table():
    centre = 1.0 + 2.0 * DIFFUSION
    root = (centre - math.sqrt(centre * centre - 4.0 * DIFFUSION * DIFFUSION)) / (2.0 * DIFFUSION)
    factor = 1.0 / (DIFFUSION * (1.0 / root - root) * (1.0 - root**LON))
    offset = np.abs(np.arange(LON)[:, None] - np.arange(LON)[None, :])
    nearest = np.minimum(offset, LON - offset).astype(np.float64)
    values = (np.exp(nearest * math.log(root)) + np.exp((LON - nearest) * math.log(root))) * factor
    table = np.zeros((LANES, LANES), np.float32)
    table[:LON, :LON] = values
    return table.astype(BF)


def row_factors():
    rows = np.arange(-HALO, TOTAL_ROWS + HALO)
    cosine = np.cos(math.pi * ((rows + 0.5) / TOTAL_ROWS - 0.5))
    metric = 1.0 / (cosine * cosine + 0.1)
    inside = (rows >= 0) & (rows < TOTAL_ROWS)
    return np.stack([metric / (2 + 2 * metric), 1 / (2 + 2 * metric), inside], axis=1).astype(np.float32)


def hot(condition):
    return jnp.where(condition, 1.0, 0.0).astype(BF)


def iota(shape, dim):
    return lax.broadcasted_iota(jnp.int32, shape, dim)


def grid_to_message(transposed):
    shape = (320, 256) if transposed else (256, 320)
    row, col = iota(shape, int(transposed)), iota(shape, 1 - int(transposed))
    group, place = row >> 4, row & 15
    main = hot(col == (place >> 2) * FIELDS + group * 5 + (place & 3))
    fifth = col == (place & 3) * FIELDS + group * 5 + 4
    return main, [hot(fifth & ((place >> 2) == t)) for t in range(TILES)]


def message_to_station(transposed):
    shape = (256, 512) if transposed else (512, 256)
    row, col = iota(shape, int(transposed)), iota(shape, 1 - int(transposed))
    r, member, f = row >> 7, (row >> 3) & 15, row & 7
    same = member == (col >> 4)
    place = col & 15
    main = hot(same & (f < 4) & (place == r * 4 + f))
    return main, [hot(same & (f == 4) & (place == t * 4 + r)) for t in range(TILES)]


def lane_tile(t):
    return slice(t * 128, (t + 1) * 128)


def lane_chunk(q):
    return slice(q * CHUNK, (q + 1) * CHUNK)


def dot(a, b):
    return jnp.dot(a, b, preferred_element_type=F32)


def dot_t(a, b):
    return lax.dot_general(a, b, (((1,), (1,)), ((), ())), preferred_element_type=F32)


def stencil_row(u, nxt, weight, row, east_west, north_south, inside):
    tiles = LANES // 128
    lane = iota((FIELDS, 128), 1)

    def tile(at, t):
        return u[at, :, t * 128 : (t + 1) * 128].astype(F32)

    first, last = tile(row, 0), tile(row, tiles - 1)
    wrapped = jnp.where(lane == LON % 128, pltpu.roll(first, LON % 128, 1), last)
    before = pltpu.roll(last, 129 - LON % 128, 1)
    here = first
    ahead = pltpu.roll(here, 127, 1)
    for pair in range(tiles // 2):
        values, middles = [], []
        for t in (2 * pair, 2 * pair + 1):
            after = wrapped if t == tiles - 2 else (tile(row, t + 1) if t < tiles - 1 else here)
            further = pltpu.roll(after, 127, 1) if t < tiles - 1 else ahead
            east = jnp.where(lane == 127, further, ahead)
            moved = pltpu.roll(here, 1, 1)
            west = jnp.where(lane == 0, before, moved)
            sides = tile(row - 1, t) + tile(row + 1, t)
            values.append((east + west) * east_west + sides * north_south - here)
            middles.append(here)
            before, here, ahead = moved, after, further
        mixed = dot(weight, jnp.concatenate(values, axis=1).astype(BF))
        fresh = jnp.concatenate(middles, axis=1) + jnp.tanh(mixed)
        if inside is not None:
            fresh = fresh * inside
        nxt[row, :, pair * 256 : (pair + 1) * 256] = fresh.astype(BF)


def diffuse_chunk(q, rows, inverse, main, fifth, message):
    piece = dot(rows, inverse[:, lane_chunk(q)]).astype(BF)
    message[q, :, :, :CHUNK] = dot(main, piece).astype(BF).reshape(MEMBERS, 16, CHUNK)
    below = sum(dot(fifth[t], piece[:, lane_tile(t)]) for t in range(TILES))
    message[q, :, :, CHUNK:] = below.astype(BF).reshape(MEMBERS, 16, 128)


def pair_terms(values, truth):
    slopes = [None] * MEMBERS
    total = None
    for i in range(MEMBERS):
        for j in range(i + 1, MEMBERS):
            spread = values[i] - values[j]
            square = spread * spread + 1.0
            inverse = lax.rsqrt(square)
            slope = spread * inverse
            root = square * inverse
            total = root if total is None else total + root
            slopes[i] = slope if slopes[i] is None else slopes[i] + slope
            slopes[j] = -slope if slopes[j] is None else slopes[j] - slope
    error_total = None
    grads = []
    for m in range(MEMBERS):
        error = values[m] - truth
        square = error * error + 1.0
        inverse = lax.rsqrt(square)
        root = square * inverse
        error_total = root if error_total is None else error_total + root
        grads.append(error * inverse - slopes[m] * (1.0 / (MEMBERS - 1)))
    score = (error_total - MEMBERS) * (1.0 / MEMBERS) - (total - PAIRS) * (1.0 / (MEMBERS * (MEMBERS - 1)))
    return score, grads


def send(src, dst, sems, at, device):
    return pltpu.make_async_remote_copy(
        src_ref=src,
        dst_ref=dst,
        send_sem=sems.at[0, at],
        recv_sem=sems.at[1, at],
        device_id=device,
        device_id_type=pl.DeviceIdType.MESH,
    )


def member_at(member, step, sign):
    x = (member + sign * (step & 3)) & 3
    y = ((member >> 2) + sign * (step >> 2)) & 3
    return y * 4 + x


def band_at(band, step, sign):
    return (band + sign * step) & (BANDS - 1)


def exchange(source, target, sems, me, at, axis):
    @pl.loop(1, 16)
    def _(step):
        peer = at(me, step, 1)
        send(source(peer), target(me), sems, step, {axis: peer}).start()


def wait_received(source, target, sems, me, at, axis):
    @pl.loop(1, 16)
    def _(step):
        peer = at(me, step, -1)
        send(source(peer), target(peer), sems, step, {axis: peer}).wait_recv()


def wait_sent(source, target, sems, me, at, axis):
    @pl.loop(1, 16)
    def _(step):
        peer = at(me, step, 1)
        send(source(peer), target(me), sems, step, {axis: peer}).wait_send()


def find_slots(band_ref, band, slot_ref):
    own = [band_ref[band * 16 + k] for k in range(16)]
    for k in range(16):
        rank = jnp.int32(0)
        for i in range(k):
            rank += jnp.where(own[i] == own[k], 1, 0)
        slot_ref[k] = own[k] * CAP + rank


def find_starts(band_ref, first_ref, band, start_ref):
    @pl.loop(0, BANDS)
    def _(home):
        seen, first, second = jnp.int32(0), jnp.int32(0), jnp.int32(0)
        for k in range(16):
            match = band_ref[home * 16 + k] == band
            here = first_ref[home * 16 + k]
            first = jnp.where(match & (seen == 0), here, first)
            second = jnp.where(match & (seen == 1), here, second)
            seen += jnp.where(match, 1, 0)
        start_ref[home * CAP] = first
        start_ref[home * CAP + 1] = second


def outgoing_shares(slot_ref, weight_ref, member, zout):
    row, col = iota((8, 128), 0), iota((8, 128), 1)
    own = hot(col == (16 + (member & 1) * 8 + row) * ROWS + ((member >> 1) & 3))
    share = jnp.concatenate([dot(own, weight_ref[k]) for k in range(16)], axis=0).astype(BF)
    lane = iota((1, 128), 1)
    slot_row = jnp.zeros((1, 128), jnp.int32)
    for k in range(16):
        slot_row = jnp.where((lane >> 3) == k, slot_ref[k], slot_row)
    row, col = iota((128, 128), 0), iota((128, 128), 1)
    pick = hot(((row >> 3) * CAP + (member >> 3) == slot_row) & ((row & 7) == (col & 7)))
    picked = dot(pick, share)
    for b in range(BANDS):
        zout[b] = jnp.concatenate([picked[b * 8 : b * 8 + 8], jnp.zeros((8, 128), F32)], axis=0).astype(BF)


def join_shares(zin, joined):
    for pair in range(BANDS // 2):
        parts = [zin[2 * pair + odd].astype(F32)[0:8] for odd in range(2)]
        joined[pair] = jnp.concatenate(parts, axis=0).astype(BF)


def outgoing_direct(slot_ref, weight_ref, turned, direct_out):
    row, col = iota((64, 128), 0), iota((64, 128), 1)
    pick = hot(col == (row & 15) * ROWS + (row >> 4))
    for k in range(16):
        turned[k] = dot(pick, weight_ref[k]).astype(BF)

    @pl.loop(0, BANDS)
    def _(b):
        for cap in range(CAP):
            block = jnp.zeros((64, 128), BF)
            for k in range(16):
                block = jnp.where(jnp.full((64, 128), slot_ref[k], jnp.int32) == b * CAP + cap, turned[k], block)
            direct_out[b, cap * 64 : (cap + 1) * 64, :] = block


def outgoing_obs(slot_ref, obs_ref, member, obs_out):
    row, col = iota((16, FIELDS), 0), iota((16, FIELDS), 1)
    pick = hot((row < 5) & (col == member * 5 + row))
    own = dot_t(pick, obs_ref[...].reshape(16 * STATIONS, FIELDS))[0:8]
    group = iota((8, 128), 1) >> 5
    blocks = []
    for k in range(16):
        block = jnp.where(group == (k & 3), own[:, lane_tile(k >> 2)], 0.0)
        block += pltpu.roll(block, 32, 1)
        blocks.append(block + pltpu.roll(block, 64, 1))
    for t in range(SLOTS // 4):
        tile = jnp.zeros((8, 128), F32)
        for k in range(16):
            tile = jnp.where(group + 4 * t == slot_ref[k], blocks[k], tile)
        for odd in range(2):
            piece = pltpu.roll(tile, 64, 1) if odd else tile
            obs_out[2 * t + odd] = jnp.concatenate([piece, jnp.zeros((8, 128), F32)], axis=0).astype(BF)


def spread_out_weights(start_ref, direct, weights, spread_weight):
    lane = iota((STATIONS, 128), 1)

    @pl.loop(0, BANDS // 2)
    def _(pair):
        for cap in range(CAP):
            shares = [
                [weights[cap * 8 + r * 2 + g, pair].astype(F32) for g in range(2)] for r in range(ROWS)
            ]
            for odd in range(2):
                home = pair * 2 + odd
                start = start_ref[home * CAP + cap]
                shift = start & 127
                at = pl.ds(home * 64 + cap * STATIONS, STATIONS)
                moved = []
                for r in range(ROWS):
                    near = direct[home, cap * 64 + r * 16 : cap * 64 + r * 16 + 16, :].astype(F32)
                    passed = [share[odd * 8 : odd * 8 + 8] for share in shares[r]]
                    moved.append(pltpu.roll(jnp.concatenate([near] + passed, axis=0), shift, 1))
                for t in range(LANES // 128):
                    place = lane + t * 128 - start
                    inside = (place >= 0) & (place < 128)
                    for r in range(ROWS):
                        spread_weight[r, at, lane_tile(t)] = jnp.where(inside, moved[r], 0.0).astype(BF)


def fold_truth(truth_ref, truth):
    truth[...] = jnp.zeros((CHUNKS, 16, PIECE), F32)
    fields = [truth_ref[f].astype(F32) for f in range(5)]
    for q in range(CHUNKS):
        width = min(CHUNK, LON - q * CHUNK)
        for r in range(ROWS):
            for f in range(4):
                truth[q, 4 * r + f : 4 * r + f + 1, :width] = fields[f][r : r + 1, q * CHUNK : q * CHUNK + width]
        for t in range(TILES):
            first = q * CHUNK + t * 128
            width = min(128, LON - first)
            truth[q, 4 * t : 4 * t + 4, CHUNK : CHUNK + width] = fields[4][:, first : first + width]


def unfold_score(score, score_ref):
    for q in range(CHUNKS):
        width = min(CHUNK, LON - q * CHUNK)
        for r in range(ROWS):
            for f in range(4):
                score_ref[f, r : r + 1, q * CHUNK : q * CHUNK + width] = score[
                    q, 4 * r + f : 4 * r + f + 1, :width
                ]
        for t in range(TILES):
            first = q * CHUNK + t * 128
            width = min(128, LON - first)
            score_ref[4, :, first : first + width] = score[q, 4 * t : 4 * t + 4, CHUNK : CHUNK + width]


def join_obs(obs_in, obs):
    lane = iota((8, 128), 1)
    for t in range(POINTS // 128):
        low = obs_in[2 * t].astype(F32)[0:8]
        high = obs_in[2 * t + 1].astype(F32)[0:8]
        obs[:, lane_tile(t)] = jnp.where(lane < 64, low, pltpu.roll(high, 64, 1))


def station_rows(q, received, main, fifth, rows):
    for t in range(TILES):
        tile = dot(main, received[q, :, :, lane_tile(t)].reshape(256, 128))
        tile += dot(fifth[t], received[q, :, :, CHUNK:].reshape(256, 128))
        rows[:, lane_tile(q * TILES + t)] = tile.astype(BF)


def estimates(first, stop, rows, spread_weight, est):
    for r in range(ROWS):
        part = dot_t(rows[r * 128 : (r + 1) * 128, first:stop], spread_weight[r, :, first:stop])
        est[...] = part if r == 0 and first == 0 else est[...] + part


def station_scores(est, slopes, obs, station_out):
    lane = iota((8, 128), 1)

    @pl.loop(0, POINTS // 256)
    def _(n):
        for half in range(2):
            at = pl.ds(pl.multiple_of(n * 256 + half * 128, 128), 128)
            members = [est[m * 8 : (m + 1) * 8, at] for m in range(MEMBERS)]
            total, grads = pair_terms(members, obs[:, at])
            other = pltpu.roll(total, 64, 1)
            station_out[4 * n + 2 * half] = jnp.where(lane < 64, total, other)
            station_out[4 * n + 2 * half + 1] = jnp.where(lane < 64, other, total)
            for m in range(0, MEMBERS, 2):
                slopes[m * 8 : m * 8 + 16, at] = jnp.concatenate(grads[m : m + 2], axis=0).astype(BF)


def grid_pairs(q, received, values, truth, score):
    values[q] = received[q].astype(F32)

    @pl.loop(0, PIECE // 128)
    def _(n):
        at = pl.ds(pl.multiple_of(n * 128, 128), 128)
        for half in range(2):
            part = slice(half * 8, half * 8 + 8)
            members = [values[q, m, part, at] for m in range(MEMBERS)]
            total, grads = pair_terms(members, truth[q, part, at])
            score[q, part, at] = total
            for m in range(MEMBERS):
                values[q, m, part, at] = grads[m]


def spread_chunk(q, slopes, spread_weight, spread):
    for r in range(ROWS):
        part = dot(slopes[...], spread_weight[r, :, lane_chunk(q)])
        spread[r * 128 : (r + 1) * 128, :] = part.astype(BF)


def total_chunk(q, values, spread, back, back_fifth, grad):
    total = values[q, :, :, :CHUNK].reshape(256, CHUNK) + dot(back, spread[...])
    grad[q, :, :, :CHUNK] = total.astype(BF).reshape(MEMBERS, 16, CHUNK)
    below = values[q, :, :, CHUNK:].reshape(256, 128)
    for t in range(TILES):
        below += dot(back_fifth[t], spread[:, lane_tile(t)])
    grad[q, :, :, CHUNK:] = below.astype(BF).reshape(MEMBERS, 16, 128)


def own_station_scores(slot_ref, station_in, own):
    group = iota((8, 128), 1) >> 5
    even = (group & 1) == 0
    pieces = []
    for b in range(BANDS):
        here = station_in[b]
        moved = pltpu.roll(here, 32, 1)
        pieces.append(jnp.where(even, here, moved))
        pieces.append(jnp.where(even, moved, here))
    tiles = []
    for t in range(4):
        slot = jnp.zeros((8, 128), jnp.int32)
        for g in range(4):
            slot = jnp.where(group == g, slot_ref[4 * t + g], slot)
        tile = jnp.zeros((8, 128), F32)
        for at in range(SLOTS):
            tile = jnp.where(slot == at, pieces[at], tile)
        tiles.append(tile)
    for t in range(2):
        own[:, lane_tile(t)] = jnp.concatenate([tiles[t], tiles[t + 2]], axis=0).astype(BF)


def all_station_scores(gathered, station_ref):
    row, col = iota((256, FIELDS), 0), iota((256, FIELDS), 1)
    field = (row >> 4) * 5 + (row & 7)
    whole = gathered[...].reshape(256, 256)
    dims = (((0,), (0,)), ((), ()))
    for half in range(2):
        pick = hot(((row & 7) < 5) & (field == col) & (((row >> 3) & 1) == half))
        joined = lax.dot_general(whole, pick, dims, preferred_element_type=F32)
        station_ref[half * 8 : half * 8 + 8] = joined.reshape(8, STATIONS, FIELDS)


def add_state(q, returned, main, fifth, inverse, total, state, out, copies):
    for t in range(TILES):
        tile = dot(main, returned[q, :, :, lane_tile(t)].reshape(256, 128))
        tile += dot(fifth[t], returned[q, :, :, CHUNK:].reshape(256, 128))
        total[:, lane_tile(t)] = tile.astype(BF)
    for n in range(CHUNKS):
        width = min(CHUNK, LON - n * CHUNK)
        at = slice(n * CHUNK, n * CHUNK + width)
        part = dot(total[...], inverse[lane_chunk(q), at])
        if q > 0:
            part += state[:, at]
        if q < CHUNKS - 1:
            state[:, at] = part
        else:
            out[0, :, :, at] = part.astype(BF).reshape(ROWS, FIELDS, width)
            copies[n].start()


def kernel(
    band_ref, first_ref, factor_ref, state_hbm, mix_ref, weight_hbm, obs_hbm, truth_hbm, inverse_hbm,
    score_ref, station_ref, out_ref,
    start_ref, slot_ref,
    state_ref, weight_ref, obs_ref, truth_ref,
    layers, inverse, zout, zin, joined, turned, direct_out, direct_in, obs_out, obs_in, weights, spread_weight, message, received, grad, returned,
    rows, est, slopes, values, spread, truth, obs, score, station_out, station_in, own, gathered,
    total, state, score_out, scores_out, out,
    fetch_sem, leave_sem, halo_sem, z_sem, obs_sem, direct_sem, weight_sem, message_sem, station_sem, own_sem, grad_sem,
):
    band = lax.axis_index("band")
    member = lax.axis_index("member")
    barrier = pltpu.get_barrier_semaphore()

    @pl.loop(1, 16)
    def _(step):
        for device in ({"member": member_at(member, step, 1)}, {"band": band_at(band, step, 1)}):
            pl.semaphore_signal(barrier, inc=1, device_id=device, device_id_type=pl.DeviceIdType.MESH)

    fetches = [
        pltpu.make_async_copy(source, target, fetch_sem.at[i])
        for i, (source, target) in enumerate(
            [(state_hbm.at[0, r], state_ref.at[0, r]) for r in range(ROWS)]
            + [
                (weight_hbm, weight_ref), (obs_hbm, obs_ref), (truth_hbm, truth_ref),
                (inverse_hbm, inverse),
            ]
        )
    ]
    for fetch in fetches:
        fetch.start()

    u = layers.at[0]
    u[HALO : HALO + ROWS, :, LON - 32 :] = jnp.zeros((ROWS, FIELDS, LANES - LON + 32), BF)

    @pl.when(band == 0)
    def _():
        u[0:HALO] = jnp.zeros((HALO, FIELDS, LANES), BF)

    @pl.when(band == BANDS - 1)
    def _():
        u[HALO + ROWS :] = jnp.zeros((HALO, FIELDS, LANES), BF)

    find_slots(band_ref, band, slot_ref)
    for fetch in fetches[:ROWS]:
        fetch.wait()
    u[HALO : HALO + ROWS, :, :LON] = state_ref[0]

    def to_north(i):
        return send(u.at[HALO + ROWS - 1 - i], u.at[HALO - 1 - i], halo_sem, i, {"band": band_at(band, 1, 1)})

    def to_south(i):
        return send(u.at[HALO + i], u.at[HALO + ROWS + i], halo_sem, HALO + i, {"band": band_at(band, 1, -1)})

    def send_halo(i):
        pl.when(band < BANDS - 1)(to_north(i).start)
        pl.when(band > 0)(to_south(i).start)

    direct_args = (lambda b: direct_out.at[b], lambda b: direct_in.at[b], direct_sem, band, band_at, "band")
    weight_args = (lambda m: joined, lambda m: weights.at[m], weight_sem, member, member_at, "member")
    z_args = (lambda b: zout.at[b], lambda b: zin.at[b], z_sem, band, band_at, "band")
    obs_args = (lambda b: obs_out.at[b], lambda b: obs_in.at[b], obs_sem, band, band_at, "band")
    station_args = (lambda b: station_out.at[b], lambda b: station_in.at[b], station_sem, band, band_at, "band")
    own_args = (lambda m: own, lambda m: gathered.at[m], own_sem, member, member_at, "member")

    def message_args(q):
        return (
            lambda m: message.at[q, m], lambda m: received.at[q, m], message_sem.at[q], member, member_at, "member"
        )

    def grad_args(q):
        return lambda m: grad.at[q, m], lambda m: returned.at[q, m], grad_sem.at[q], member, member_at, "member"

    def run_pair(layer, low, high):
        own = HALO <= low and high < HALO + ROWS

        @pl.loop(0, 2)
        def _(side):
            row = low + side * (high - low)
            factor = band * ROWS + row
            stencil_row(
                layers.at[layer], layers.at[layer + 1], mix_ref[layer], row,
                factor_ref[factor, 0], factor_ref[factor, 1], None if own else factor_ref[factor, 2],
            )

    def wait_halo(i):
        pl.when(band > 0)(to_north(i).wait_recv)
        pl.when(band < BANDS - 1)(to_south(i).wait_recv)

    run_pair(0, 4, 5)
    fetches[ROWS].wait()
    pl.semaphore_wait(barrier, 30)
    send_halo(0)
    outgoing_shares(slot_ref, weight_ref, member, zout)
    exchange(*z_args)
    send_halo(1)
    send_halo(2)
    zin[band] = zout[band]
    fetches[ROWS + 1].wait()
    outgoing_obs(slot_ref, obs_ref, member, obs_out)
    obs_in[band] = obs_out[band]
    outgoing_direct(slot_ref, weight_ref, turned, direct_out)
    direct_in[band] = direct_out[band]
    find_starts(band_ref, first_ref, band, start_ref)
    fetches[ROWS + 2].wait()
    fold_truth(truth_ref, truth)
    wait_halo(0)
    run_pair(0, 3, 6)
    wait_received(*z_args)
    join_shares(zin, joined)
    exchange(*weight_args)
    weights[member] = joined[...]
    run_pair(1, 4, 5)
    wait_halo(1)
    exchange(*obs_args)
    exchange(*direct_args)
    run_pair(0, 2, 7)
    run_pair(1, 3, 6)
    run_pair(2, 4, 5)
    wait_halo(2)
    run_pair(0, 1, 8)
    run_pair(1, 2, 7)
    run_pair(2, 3, 6)

    fetches[ROWS + 3].wait()
    main, fifth = grid_to_message(False)
    grid_rows = layers[LAYERS, HALO : HALO + ROWS].reshape(ROWS * FIELDS, LANES)
    for q in range(CHUNKS):
        diffuse_chunk(q, grid_rows, inverse, main, fifth, message)
        exchange(*message_args(q))
        received[q, member] = message[q, member]

    main, fifth = message_to_station(False)
    for q in range(CHUNKS - 1):
        wait_received(*message_args(q))
        station_rows(q, received, main, fifth, rows)
        grid_pairs(q, received, values, truth, score)
        if q == 0:
            wait_received(*obs_args)
            join_obs(obs_in, obs)
            wait_received(*weight_args)
            wait_received(*direct_args)
            spread_out_weights(start_ref, direct_in, weights, spread_weight)

    estimates(0, CHUNK * (CHUNKS - 1), rows, spread_weight, est)
    wait_received(*message_args(CHUNKS - 1))
    station_rows(CHUNKS - 1, received, main, fifth, rows)
    estimates(CHUNK * (CHUNKS - 1), LANES, rows, spread_weight, est)
    station_scores(est, slopes, obs, station_out)
    exchange(*station_args)
    station_in[band] = station_out[band]

    def share_station_scores():
        wait_received(*station_args)
        own_station_scores(slot_ref, station_in, own)
        exchange(*own_args)
        gathered[member] = own[...]

    back, back_fifth = message_to_station(True)
    for q in range(CHUNKS):
        spread_chunk(q, slopes, spread_weight, spread)
        if q == CHUNKS - 1:
            grid_pairs(q, received, values, truth, score)
        total_chunk(q, values, spread, back, back_fifth, grad)
        exchange(*grad_args(q))
        returned[q, member] = grad[q, member]

    leave = [
        pltpu.make_async_copy(score_out, score_ref, leave_sem.at[0]),
        pltpu.make_async_copy(scores_out, station_ref, leave_sem.at[1]),
    ]
    leave_state = []
    for n in range(CHUNKS):
        at = slice(n * CHUNK, min((n + 1) * CHUNK, LON))
        leave_state.append(pltpu.make_async_copy(out.at[:, :, :, at], out_ref.at[:, :, :, at], leave_sem.at[2 + n]))
    unfold_score(score, score_out)
    leave[0].start()
    share_station_scores()
    for i in range(HALO):
        pl.when(band < BANDS - 1)(to_north(i).wait_send)
        pl.when(band > 0)(to_south(i).wait_send)
    for args in (obs_args, z_args, direct_args, weight_args, station_args):
        wait_sent(*args)
    for q in range(CHUNKS):
        wait_sent(*message_args(q))

    main, fifth = grid_to_message(True)
    for q in range(CHUNKS):
        wait_received(*grad_args(q))
        add_state(q, returned, main, fifth, inverse, total, state, out, leave_state)
        wait_sent(*grad_args(q))
    wait_received(*own_args)
    all_station_scores(gathered, scores_out)
    leave[1].start()
    wait_sent(*own_args)
    for copy in leave:
        copy.wait()
    for copy in leave_state:
        copy.wait()


def hand_over(*refs):
    count = len(refs) // 2
    for i in range(count):
        refs[count + i][...] = refs[i][...]


def shards(ensemble, mix_weight, analysis, station_weight, station_obs, block_band, block_start):
    smem = pl.BlockSpec(memory_space=pltpu.SMEM)
    vmem = pl.BlockSpec(memory_space=pltpu.VMEM)
    anywhere = pl.BlockSpec(memory_space=pl.ANY)
    message = (CHUNKS, MEMBERS, 16, PIECE)
    sems = pltpu.SemaphoreType.DMA((2, 16))
    piece_sems = pltpu.SemaphoreType.DMA((CHUNKS, 2, 16))
    shapes = (
        jax.ShapeDtypeStruct((5, ROWS, LON), F32),
        jax.ShapeDtypeStruct((16, STATIONS, FIELDS), F32),
        jax.ShapeDtypeStruct((1, ROWS, FIELDS, LON), BF),
    )
    outs = pl.pallas_call(
        kernel,
        out_shape=tuple(pltpu.VMEM(shape.shape, shape.dtype) for shape in shapes),
        in_specs=[smem] * 3 + [anywhere, vmem] + [anywhere] * 4,
        out_specs=(anywhere,) * 3,
        scratch_shapes=[
            pltpu.SMEM((SLOTS,), jnp.int32),
            pltpu.SMEM((16,), jnp.int32),
            pltpu.VMEM((1, ROWS, FIELDS, LON), BF),
            pltpu.VMEM((16, STATIONS * ROWS, 128), BF),
            pltpu.VMEM((16, STATIONS, FIELDS), BF),
            pltpu.VMEM((5, ROWS, LON), BF),
            pltpu.VMEM((LAYERS + 1, EXT, FIELDS, LANES), BF),
            pltpu.VMEM((LANES, LANES), BF),
            pltpu.VMEM((BANDS, 16, 128), BF),
            pltpu.VMEM((BANDS, 16, 128), BF),
            pltpu.VMEM((BANDS // 2, 16, 128), BF),
            pltpu.VMEM((16, 64, 128), BF),
            pltpu.VMEM((BANDS, 128, 128), BF),
            pltpu.VMEM((BANDS, 128, 128), BF),
            pltpu.VMEM((BANDS, 16, 128), BF),
            pltpu.VMEM((BANDS, 16, 128), BF),
            pltpu.VMEM((MEMBERS, BANDS // 2, 16, 128), BF),
            pltpu.VMEM((ROWS, POINTS, LANES), BF),
            pltpu.VMEM(message, BF),
            pltpu.VMEM(message, BF),
            pltpu.VMEM(message, BF),
            pltpu.VMEM(message, BF),
            pltpu.VMEM((512, LANES), BF),
            pltpu.VMEM((128, POINTS), F32),
            pltpu.VMEM((128, POINTS), BF),
            pltpu.VMEM(message, F32),
            pltpu.VMEM((512, CHUNK), BF),
            pltpu.VMEM((CHUNKS, 16, PIECE), F32),
            pltpu.VMEM((8, POINTS), F32),
            pltpu.VMEM((CHUNKS, 16, PIECE), F32),
            pltpu.VMEM((BANDS, 8, 128), F32),
            pltpu.VMEM((BANDS, 8, 128), F32),
            pltpu.VMEM((16, 256), BF),
            pltpu.VMEM((MEMBERS, 16, 256), BF),
            pltpu.VMEM((ROWS * FIELDS, CHUNK), BF),
            pltpu.VMEM((ROWS * FIELDS, LON), F32),
            pltpu.VMEM((5, ROWS, LON), F32),
            pltpu.VMEM((16, STATIONS, FIELDS), F32),
            pltpu.VMEM((1, ROWS, FIELDS, LON), BF),
            pltpu.SemaphoreType.DMA((ROWS + 4,)),
            pltpu.SemaphoreType.DMA((2 + CHUNKS,)),
            sems, sems, sems, sems, sems, piece_sems, sems, sems, piece_sems,
        ],
        compiler_params=pltpu.CompilerParams(
            vmem_limit_bytes=56 * MIB, collective_id=0, has_side_effects=True
        ),
    )(
        block_band.reshape(-1), block_start, jnp.asarray(row_factors()), ensemble, mix_weight,
        station_weight.reshape(16, STATIONS * ROWS, 128),        station_obs, jnp.transpose(analysis, (1, 0, 2)), jnp.asarray(inverse_table()),
    )
    score, station, state = pl.pallas_call(
        hand_over,
        out_shape=shapes,
        in_specs=[vmem] * 3,
        out_specs=(vmem,) * 3,
        compiler_params=pltpu.CompilerParams(vmem_limit_bytes=16 * MIB),
    )(*outs)
    return jnp.transpose(score, (1, 0, 2)), station, state


def solution(mesh):
    return jax.shard_map(
        shards,
        mesh=mesh,
        in_specs=(
            P("member", "band", None, None),
            P(),
            P("band", "member", None),
            P("band", None, None, None),
            P("band", None, None),
            P(),
            P(),
        ),
        out_specs=(
            P("band", "member", None),
            P("band", None, None),
            P("member", "band", None, None),
        ),
        check_vma=False,
    )
```

```python
import math

import jax
import jax.numpy as jnp
import numpy as np
from jax import lax
from jax.experimental import pallas as pl
from jax.experimental.pallas import tpu as pltpu
from jax.sharding import PartitionSpec as P

CAP = 2
DIFFUSION = 4.0

ROWS = 4
HALO = 3
EXT = ROWS + 2 * HALO
FIELDS = 80
LON = 1440
LANES = 1536
CHUNKS = 3
CHUNK = LANES // CHUNKS
TILES = CHUNK // 128
PIECE = CHUNK + 128
MEMBERS = 16
BANDS = 16
TOTAL_ROWS = 64
LAYERS = 3
SLOTS = BANDS * CAP
STATIONS = 32
POINTS = SLOTS * STATIONS
PAIRS = MEMBERS * (MEMBERS - 1) // 2
MIB = 1 << 20

BF = jnp.bfloat16
F32 = jnp.float32


def inverse_table():
    centre = 1.0 + 2.0 * DIFFUSION
    root = (centre - math.sqrt(centre * centre - 4.0 * DIFFUSION * DIFFUSION)) / (2.0 * DIFFUSION)
    factor = 1.0 / (DIFFUSION * (1.0 / root - root) * (1.0 - root**LON))
    offset = np.abs(np.arange(LON)[:, None] - np.arange(LON)[None, :])
    nearest = np.minimum(offset, LON - offset).astype(np.float64)
    values = (np.exp(nearest * math.log(root)) + np.exp((LON - nearest) * math.log(root))) * factor
    table = np.zeros((LANES, LANES), np.float32)
    table[:LON, :LON] = values
    return table.astype(BF)


def row_factors():
    rows = np.arange(-HALO, TOTAL_ROWS + HALO)
    cosine = np.cos(math.pi * ((rows + 0.5) / TOTAL_ROWS - 0.5))
    metric = 1.0 / (cosine * cosine + 0.1)
    inside = (rows >= 0) & (rows < TOTAL_ROWS)
    return np.stack([metric / (2 + 2 * metric), 1 / (2 + 2 * metric), inside], axis=1).astype(np.float32)


def hot(condition):
    return jnp.where(condition, 1.0, 0.0).astype(BF)


def iota(shape, dim):
    return lax.broadcasted_iota(jnp.int32, shape, dim)


def grid_to_message(transposed):
    shape = (320, 256) if transposed else (256, 320)
    row, col = iota(shape, int(transposed)), iota(shape, 1 - int(transposed))
    group, place = row >> 4, row & 15
    main = hot(col == (place >> 2) * FIELDS + group * 5 + (place & 3))
    fifth = col == (place & 3) * FIELDS + group * 5 + 4
    return main, [hot(fifth & ((place >> 2) == t)) for t in range(TILES)]


def message_to_station(transposed):
    shape = (256, 512) if transposed else (512, 256)
    row, col = iota(shape, int(transposed)), iota(shape, 1 - int(transposed))
    r, member, f = row >> 7, (row >> 3) & 15, row & 7
    same = member == (col >> 4)
    place = col & 15
    main = hot(same & (f < 4) & (place == r * 4 + f))
    return main, [hot(same & (f == 4) & (place == t * 4 + r)) for t in range(TILES)]


def lane_tile(t):
    return slice(t * 128, (t + 1) * 128)


def lane_chunk(q):
    return slice(q * CHUNK, (q + 1) * CHUNK)


def dot(a, b):
    return jnp.dot(a, b, preferred_element_type=F32)


def dot_t(a, b):
    return lax.dot_general(a, b, (((1,), (1,)), ((), ())), preferred_element_type=F32)


def stencil_row(u, nxt, weight, row, east_west, north_south, inside):
    tiles = LANES // 128
    lane = iota((FIELDS, 128), 1)

    def tile(at, t):
        return u[at, :, t * 128 : (t + 1) * 128].astype(F32)

    first, last = tile(row, 0), tile(row, tiles - 1)
    wrapped = jnp.where(lane == LON % 128, pltpu.roll(first, LON % 128, 1), last)
    before = pltpu.roll(last, 129 - LON % 128, 1)
    here = first
    ahead = pltpu.roll(here, 127, 1)
    for pair in range(tiles // 2):
        values, middles = [], []
        for t in (2 * pair, 2 * pair + 1):
            after = wrapped if t == tiles - 2 else (tile(row, t + 1) if t < tiles - 1 else here)
            further = pltpu.roll(after, 127, 1) if t < tiles - 1 else ahead
            east = jnp.where(lane == 127, further, ahead)
            moved = pltpu.roll(here, 1, 1)
            west = jnp.where(lane == 0, before, moved)
            sides = tile(row - 1, t) + tile(row + 1, t)
            values.append((east + west) * east_west + sides * north_south - here)
            middles.append(here)
            before, here, ahead = moved, after, further
        mixed = dot(weight, jnp.concatenate(values, axis=1).astype(BF))
        fresh = jnp.concatenate(middles, axis=1) + jnp.tanh(mixed)
        if inside is not None:
            fresh = fresh * inside
        nxt[row, :, pair * 256 : (pair + 1) * 256] = fresh.astype(BF)


def diffuse_chunk(q, rows, inverse, main, fifth, message):
    piece = dot(rows, inverse[:, lane_chunk(q)]).astype(BF)
    message[q, :, :, :CHUNK] = dot(main, piece).astype(BF).reshape(MEMBERS, 16, CHUNK)
    below = sum(dot(fifth[t], piece[:, lane_tile(t)]) for t in range(TILES))
    message[q, :, :, CHUNK:] = below.astype(BF).reshape(MEMBERS, 16, 128)


def pair_terms(values, truth):
    slopes = [None] * MEMBERS
    total = None
    for i in range(MEMBERS):
        for j in range(i + 1, MEMBERS):
            spread = values[i] - values[j]
            square = spread * spread + 1.0
            inverse = lax.rsqrt(square)
            slope = spread * inverse
            root = square * inverse
            total = root if total is None else total + root
            slopes[i] = slope if slopes[i] is None else slopes[i] + slope
            slopes[j] = -slope if slopes[j] is None else slopes[j] - slope
    error_total = None
    grads = []
    for m in range(MEMBERS):
        error = values[m] - truth
        square = error * error + 1.0
        inverse = lax.rsqrt(square)
        root = square * inverse
        error_total = root if error_total is None else error_total + root
        grads.append(error * inverse - slopes[m] * (1.0 / (MEMBERS - 1)))
    score = (error_total - MEMBERS) * (1.0 / MEMBERS) - (total - PAIRS) * (1.0 / (MEMBERS * (MEMBERS - 1)))
    return score, grads


def send(src, dst, sems, device):
    return pltpu.make_async_remote_copy(
        src_ref=src,
        dst_ref=dst,
        send_sem=sems.at[0],
        recv_sem=sems.at[1],
        device_id=device,
        device_id_type=pl.DeviceIdType.MESH,
    )


def member_at(member, step, sign):
    x = (member + sign * (step & 3)) & 3
    y = ((member >> 2) + sign * (step >> 2)) & 3
    return y * 4 + x


def band_at(band, step, sign):
    return (band + sign * step) & (BANDS - 1)


def exchange(source, target, sems, me, at, axis):
    @pl.loop(1, 16)
    def _(step):
        peer = at(me, step, 1)
        send(source(peer), target.at[me], sems, {axis: peer}).start()


def all_others(target, sems, me, at, axis):
    whole = target.at[0:15]
    return send(whole, whole, sems, {axis: at(me, 1, 1)})


def wait_received(source, target, sems, me, at, axis):
    all_others(target, sems, me, at, axis).wait_recv()


def wait_sent(source, target, sems, me, at, axis):
    all_others(target, sems, me, at, axis).wait_send()


def find_slots(band_ref, band, slot_ref):
    own = [band_ref[band * 16 + k] for k in range(16)]
    for k in range(16):
        rank = jnp.int32(0)
        for i in range(k):
            rank += jnp.where(own[i] == own[k], 1, 0)
        slot_ref[k] = own[k] * CAP + rank


def find_starts(band_ref, first_ref, band, start_ref):
    @pl.loop(0, BANDS)
    def _(home):
        seen, first, second = jnp.int32(0), jnp.int32(0), jnp.int32(0)
        for k in range(16):
            match = band_ref[home * 16 + k] == band
            here = first_ref[home * 16 + k]
            first = jnp.where(match & (seen == 0), here, first)
            second = jnp.where(match & (seen == 1), here, second)
            seen += jnp.where(match, 1, 0)
        start_ref[home * CAP] = first
        start_ref[home * CAP + 1] = second


def outgoing_shares(slot_ref, weight_ref, member, zout):
    row, col = iota((8, 128), 0), iota((8, 128), 1)
    own = hot(col == (16 + (member & 1) * 8 + row) * ROWS + ((member >> 1) & 3))
    share = jnp.concatenate([dot(own, weight_ref[k]) for k in range(16)], axis=0).astype(BF)
    lane = iota((1, 128), 1)
    slot_row = jnp.zeros((1, 128), jnp.int32)
    for k in range(16):
        slot_row = jnp.where((lane >> 3) == k, slot_ref[k], slot_row)
    row, col = iota((128, 128), 0), iota((128, 128), 1)
    pick = hot(((row >> 3) * CAP + (member >> 3) == slot_row) & ((row & 7) == (col & 7)))
    picked = dot(pick, share)
    for b in range(BANDS):
        zout[b] = jnp.concatenate([picked[b * 8 : b * 8 + 8], jnp.zeros((8, 128), F32)], axis=0).astype(BF)


def join_shares(zin, joined):
    for pair in range(BANDS // 2):
        parts = [zin[2 * pair + odd].astype(F32)[0:8] for odd in range(2)]
        joined[pair] = jnp.concatenate(parts, axis=0).astype(BF)


def outgoing_direct(slot_ref, weight_ref, turned, direct_out):
    row, col = iota((64, 128), 0), iota((64, 128), 1)
    pick = hot(col == (row & 15) * ROWS + (row >> 4))
    for k in range(16):
        turned[k] = dot(pick, weight_ref[k]).astype(BF)

    @pl.loop(0, BANDS)
    def _(b):
        for cap in range(CAP):
            block = jnp.zeros((64, 128), BF)
            for k in range(16):
                block = jnp.where(jnp.full((64, 128), slot_ref[k], jnp.int32) == b * CAP + cap, turned[k], block)
            direct_out[b, cap * 64 : (cap + 1) * 64, :] = block


def outgoing_obs(slot_ref, obs_ref, member, obs_out):
    row, col = iota((16, FIELDS), 0), iota((16, FIELDS), 1)
    pick = hot((row < 5) & (col == member * 5 + row))
    own = dot_t(pick, obs_ref[...].reshape(16 * STATIONS, FIELDS))[0:8]
    group = iota((8, 128), 1) >> 5
    blocks = []
    for k in range(16):
        block = jnp.where(group == (k & 3), own[:, lane_tile(k >> 2)], 0.0)
        block += pltpu.roll(block, 32, 1)
        blocks.append(block + pltpu.roll(block, 64, 1))
    for t in range(SLOTS // 4):
        tile = jnp.zeros((8, 128), F32)
        for k in range(16):
            tile = jnp.where(group + 4 * t == slot_ref[k], blocks[k], tile)
        for odd in range(2):
            piece = pltpu.roll(tile, 64, 1) if odd else tile
            obs_out[2 * t + odd] = jnp.concatenate([piece, jnp.zeros((8, 128), F32)], axis=0).astype(BF)


def spread_out_weights(start_ref, direct, weights, spread_weight):
    lane = iota((STATIONS, 128), 1)

    @pl.loop(0, BANDS // 2)
    def _(pair):
        for cap in range(CAP):
            shares = [
                [weights[cap * 8 + r * 2 + g, pair].astype(F32) for g in range(2)] for r in range(ROWS)
            ]
            for odd in range(2):
                home = pair * 2 + odd
                start = start_ref[home * CAP + cap]
                shift = start & 127
                at = pl.ds(home * 64 + cap * STATIONS, STATIONS)
                moved = []
                for r in range(ROWS):
                    near = direct[home, cap * 64 + r * 16 : cap * 64 + r * 16 + 16, :].astype(F32)
                    passed = [share[odd * 8 : odd * 8 + 8] for share in shares[r]]
                    moved.append(pltpu.roll(jnp.concatenate([near] + passed, axis=0), shift, 1))
                for t in range(LANES // 128):
                    place = lane + t * 128 - start
                    inside = (place >= 0) & (place < 128)
                    for r in range(ROWS):
                        spread_weight[r, at, lane_tile(t)] = jnp.where(inside, moved[r], 0.0).astype(BF)


def fold_truth(truth_ref, truth):
    truth[...] = jnp.zeros((CHUNKS, 16, PIECE), F32)
    fields = [truth_ref[f].astype(F32) for f in range(5)]
    for q in range(CHUNKS):
        width = min(CHUNK, LON - q * CHUNK)
        for r in range(ROWS):
            for f in range(4):
                truth[q, 4 * r + f : 4 * r + f + 1, :width] = fields[f][r : r + 1, q * CHUNK : q * CHUNK + width]
        for t in range(TILES):
            first = q * CHUNK + t * 128
            width = min(128, LON - first)
            truth[q, 4 * t : 4 * t + 4, CHUNK : CHUNK + width] = fields[4][:, first : first + width]


def unfold_score(score, score_ref):
    for q in range(CHUNKS):
        width = min(CHUNK, LON - q * CHUNK)
        for r in range(ROWS):
            for f in range(4):
                score_ref[f, r : r + 1, q * CHUNK : q * CHUNK + width] = score[
                    q, 4 * r + f : 4 * r + f + 1, :width
                ]
        for t in range(TILES):
            first = q * CHUNK + t * 128
            width = min(128, LON - first)
            score_ref[4, :, first : first + width] = score[q, 4 * t : 4 * t + 4, CHUNK : CHUNK + width]


def join_obs(obs_in, obs):
    lane = iota((8, 128), 1)
    for t in range(POINTS // 128):
        low = obs_in[2 * t].astype(F32)[0:8]
        high = obs_in[2 * t + 1].astype(F32)[0:8]
        obs[:, lane_tile(t)] = jnp.where(lane < 64, low, pltpu.roll(high, 64, 1))


def station_rows(q, received, main, fifth, rows):
    for t in range(TILES):
        tile = dot(main, received[q, :, :, lane_tile(t)].reshape(256, 128))
        tile += dot(fifth[t], received[q, :, :, CHUNK:].reshape(256, 128))
        rows[:, lane_tile(q * TILES + t)] = tile.astype(BF)


def estimates(first, stop, rows, spread_weight, est):
    for r in range(ROWS):
        part = dot_t(rows[r * 128 : (r + 1) * 128, first:stop], spread_weight[r, :, first:stop])
        est[...] = part if r == 0 and first == 0 else est[...] + part


def station_scores(est, slopes, obs, station_out):
    lane = iota((8, 128), 1)

    @pl.loop(0, POINTS // 256)
    def _(n):
        for half in range(2):
            at = pl.ds(pl.multiple_of(n * 256 + half * 128, 128), 128)
            members = [est[m * 8 : (m + 1) * 8, at] for m in range(MEMBERS)]
            total, grads = pair_terms(members, obs[:, at])
            other = pltpu.roll(total, 64, 1)
            station_out[4 * n + 2 * half] = jnp.where(lane < 64, total, other)
            station_out[4 * n + 2 * half + 1] = jnp.where(lane < 64, other, total)
            for m in range(0, MEMBERS, 2):
                slopes[m * 8 : m * 8 + 16, at] = jnp.concatenate(grads[m : m + 2], axis=0).astype(BF)


def grid_pairs(q, received, values, truth, score):
    values[q] = received[q].astype(F32)

    @pl.loop(0, PIECE // 128)
    def _(n):
        at = pl.ds(pl.multiple_of(n * 128, 128), 128)
        for half in range(2):
            part = slice(half * 8, half * 8 + 8)
            members = [values[q, m, part, at] for m in range(MEMBERS)]
            total, grads = pair_terms(members, truth[q, part, at])
            score[q, part, at] = total
            for m in range(MEMBERS):
                values[q, m, part, at] = grads[m]


def spread_chunk(q, slopes, spread_weight, spread):
    for r in range(ROWS):
        part = dot(slopes[...], spread_weight[r, :, lane_chunk(q)])
        spread[r * 128 : (r + 1) * 128, :] = part.astype(BF)


def total_chunk(q, values, spread, back, back_fifth, grad):
    total = values[q, :, :, :CHUNK].reshape(256, CHUNK) + dot(back, spread[...])
    grad[q, :, :, :CHUNK] = total.astype(BF).reshape(MEMBERS, 16, CHUNK)
    below = values[q, :, :, CHUNK:].reshape(256, 128)
    for t in range(TILES):
        below += dot(back_fifth[t], spread[:, lane_tile(t)])
    grad[q, :, :, CHUNK:] = below.astype(BF).reshape(MEMBERS, 16, 128)


def own_station_scores(slot_ref, station_in, own):
    group = iota((8, 128), 1) >> 5
    even = (group & 1) == 0
    pieces = []
    for b in range(BANDS):
        here = station_in[b]
        moved = pltpu.roll(here, 32, 1)
        pieces.append(jnp.where(even, here, moved))
        pieces.append(jnp.where(even, moved, here))
    tiles = []
    for t in range(4):
        slot = jnp.zeros((8, 128), jnp.int32)
        for g in range(4):
            slot = jnp.where(group == g, slot_ref[4 * t + g], slot)
        tile = jnp.zeros((8, 128), F32)
        for at in range(SLOTS):
            tile = jnp.where(slot == at, pieces[at], tile)
        tiles.append(tile)
    for t in range(2):
        own[:, lane_tile(t)] = jnp.concatenate([tiles[t], tiles[t + 2]], axis=0).astype(BF)


def all_station_scores(gathered, station_ref):
    row, col = iota((256, FIELDS), 0), iota((256, FIELDS), 1)
    field = (row >> 4) * 5 + (row & 7)
    whole = gathered[...].reshape(256, 256)
    dims = (((0,), (0,)), ((), ()))
    for half in range(2):
        pick = hot(((row & 7) < 5) & (field == col) & (((row >> 3) & 1) == half))
        joined = lax.dot_general(whole, pick, dims, preferred_element_type=F32)
        station_ref[half * 8 : half * 8 + 8] = joined.reshape(8, STATIONS, FIELDS)


def add_state(q, returned, main, fifth, inverse, total, state, out, copies):
    for t in range(TILES):
        tile = dot(main, returned[q, :, :, lane_tile(t)].reshape(256, 128))
        tile += dot(fifth[t], returned[q, :, :, CHUNK:].reshape(256, 128))
        total[:, lane_tile(t)] = tile.astype(BF)
    for n in range(CHUNKS):
        width = min(CHUNK, LON - n * CHUNK)
        at = slice(n * CHUNK, n * CHUNK + width)
        part = dot(total[...], inverse[lane_chunk(q), at])
        if q > 0:
            part += state[:, at]
        if q < CHUNKS - 1:
            state[:, at] = part
        else:
            out[0, :, :, at] = part.astype(BF).reshape(ROWS, FIELDS, width)
            copies[n].start()


def kernel(
    band_ref, first_ref, factor_ref, state_hbm, mix_ref, weight_hbm, obs_hbm, truth_hbm, inverse_hbm,
    score_ref, station_ref, out_ref,
    start_ref, slot_ref,
    state_ref, weight_ref, obs_ref, truth_ref,
    layers, inverse, zout, zin, joined, turned, direct_out, direct_in, obs_out, obs_in, weights, spread_weight, message, received, grad, returned,
    rows, est, slopes, values, spread, truth, obs, score, station_out, station_in, own, gathered,
    total, state, score_out, scores_out, out,
    fetch_sem, leave_sem, halo_sem, z_sem, obs_sem, direct_sem, weight_sem, message_sem, station_sem, own_sem, grad_sem,
):
    band = lax.axis_index("band")
    member = lax.axis_index("member")
    barrier = pltpu.get_barrier_semaphore()

    @pl.loop(1, 16)
    def _(step):
        for device in ({"member": member_at(member, step, 1)}, {"band": band_at(band, step, 1)}):
            pl.semaphore_signal(barrier, inc=1, device_id=device, device_id_type=pl.DeviceIdType.MESH)

    fetches = [
        pltpu.make_async_copy(source, target, fetch_sem.at[i])
        for i, (source, target) in enumerate(
            [(state_hbm.at[0, r], state_ref.at[0, r]) for r in range(ROWS)]
            + [
                (weight_hbm, weight_ref), (obs_hbm, obs_ref), (truth_hbm, truth_ref),
                (inverse_hbm, inverse),
            ]
        )
    ]
    for fetch in fetches:
        fetch.start()

    u = layers.at[0]
    u[HALO : HALO + ROWS, :, LON - 32 :] = jnp.zeros((ROWS, FIELDS, LANES - LON + 32), BF)

    @pl.when(band == 0)
    def _():
        u[0:HALO] = jnp.zeros((HALO, FIELDS, LANES), BF)

    @pl.when(band == BANDS - 1)
    def _():
        u[HALO + ROWS :] = jnp.zeros((HALO, FIELDS, LANES), BF)

    find_slots(band_ref, band, slot_ref)
    for fetch in fetches[:ROWS]:
        fetch.wait()
    u[HALO : HALO + ROWS, :, :LON] = state_ref[0]

    def to_north(i):
        return send(u.at[HALO + ROWS - 1 - i], u.at[HALO - 1 - i], halo_sem.at[i], {"band": band_at(band, 1, 1)})

    def to_south(i):
        return send(u.at[HALO + i], u.at[HALO + ROWS + i], halo_sem.at[HALO + i], {"band": band_at(band, 1, -1)})

    def send_halo(i):
        pl.when(band < BANDS - 1)(to_north(i).start)
        pl.when(band > 0)(to_south(i).start)

    direct_args = (lambda b: direct_out.at[b], direct_in, direct_sem, band, band_at, "band")
    weight_args = (lambda m: joined, weights, weight_sem, member, member_at, "member")
    z_args = (lambda b: zout.at[b], zin, z_sem, band, band_at, "band")
    obs_args = (lambda b: obs_out.at[b], obs_in, obs_sem, band, band_at, "band")
    station_args = (lambda b: station_out.at[b], station_in, station_sem, band, band_at, "band")
    own_args = (lambda m: own, gathered, own_sem, member, member_at, "member")

    def message_args(q):
        return lambda m: message.at[q, m], received.at[q], message_sem.at[q], member, member_at, "member"

    def grad_args(q):
        return lambda m: grad.at[q, m], returned.at[q], grad_sem.at[q], member, member_at, "member"

    def run_pair(layer, low, high):
        own = HALO <= low and high < HALO + ROWS
        for row in (low, high):
            factor = band * ROWS + row
            stencil_row(
                layers.at[layer], layers.at[layer + 1], mix_ref[layer], row,
                factor_ref[factor, 0], factor_ref[factor, 1], None if own else factor_ref[factor, 2],
            )

    def wait_halo(i):
        pl.when(band > 0)(to_north(i).wait_recv)
        pl.when(band < BANDS - 1)(to_south(i).wait_recv)

    run_pair(0, 4, 5)
    fetches[ROWS].wait()
    outgoing_shares(slot_ref, weight_ref, member, zout)
    fetches[ROWS + 1].wait()
    outgoing_obs(slot_ref, obs_ref, member, obs_out)
    outgoing_direct(slot_ref, weight_ref, turned, direct_out)
    pl.semaphore_wait(barrier, 30)
    send_halo(0)
    exchange(*z_args)
    send_halo(1)
    send_halo(2)
    zin[band] = zout[band]
    obs_in[band] = obs_out[band]
    direct_in[band] = direct_out[band]
    find_starts(band_ref, first_ref, band, start_ref)
    fetches[ROWS + 2].wait()
    fold_truth(truth_ref, truth)
    wait_halo(0)
    run_pair(0, 3, 6)
    run_pair(1, 4, 5)
    wait_received(*z_args)
    join_shares(zin, joined)
    exchange(*weight_args)
    weights[member] = joined[...]
    wait_halo(1)
    run_pair(0, 2, 7)
    exchange(*obs_args)
    exchange(*direct_args)
    run_pair(1, 3, 6)
    run_pair(2, 4, 5)
    wait_halo(2)
    run_pair(0, 1, 8)
    run_pair(1, 2, 7)
    run_pair(2, 3, 6)

    fetches[ROWS + 3].wait()
    main, fifth = grid_to_message(False)
    grid_rows = layers[LAYERS, HALO : HALO + ROWS].reshape(ROWS * FIELDS, LANES)
    for q in range(CHUNKS):
        diffuse_chunk(q, grid_rows, inverse, main, fifth, message)
        exchange(*message_args(q))
        received[q, member] = message[q, member]

    main, fifth = message_to_station(False)
    for q in range(CHUNKS - 1):
        wait_received(*message_args(q))
        station_rows(q, received, main, fifth, rows)
        if q == 0:
            grid_pairs(q, received, values, truth, score)
        else:
            wait_received(*obs_args)
            join_obs(obs_in, obs)
            wait_received(*weight_args)
            wait_received(*direct_args)
            spread_out_weights(start_ref, direct_in, weights, spread_weight)

    estimates(0, CHUNK * (CHUNKS - 1), rows, spread_weight, est)
    wait_received(*message_args(CHUNKS - 1))
    station_rows(CHUNKS - 1, received, main, fifth, rows)
    estimates(CHUNK * (CHUNKS - 1), LANES, rows, spread_weight, est)
    station_scores(est, slopes, obs, station_out)
    exchange(*station_args)
    station_in[band] = station_out[band]

    def share_station_scores():
        wait_received(*station_args)
        own_station_scores(slot_ref, station_in, own)
        exchange(*own_args)
        gathered[member] = own[...]

    back, back_fifth = message_to_station(True)
    for q in range(CHUNKS):
        spread_chunk(q, slopes, spread_weight, spread)
        if q > 0:
            grid_pairs(q, received, values, truth, score)
        total_chunk(q, values, spread, back, back_fifth, grad)
        exchange(*grad_args(q))
        returned[q, member] = grad[q, member]

    leave = [
        pltpu.make_async_copy(score_out, score_ref, leave_sem.at[0]),
        pltpu.make_async_copy(scores_out, station_ref, leave_sem.at[1]),
    ]
    leave_state = []
    for n in range(CHUNKS):
        at = slice(n * CHUNK, min((n + 1) * CHUNK, LON))
        leave_state.append(pltpu.make_async_copy(out.at[:, :, :, at], out_ref.at[:, :, :, at], leave_sem.at[2 + n]))
    unfold_score(score, score_out)
    leave[0].start()
    share_station_scores()
    for i in range(HALO):
        pl.when(band < BANDS - 1)(to_north(i).wait_send)
        pl.when(band > 0)(to_south(i).wait_send)
    for args in (obs_args, z_args, direct_args, weight_args, station_args):
        wait_sent(*args)
    for q in range(CHUNKS):
        wait_sent(*message_args(q))

    main, fifth = grid_to_message(True)
    for q in range(CHUNKS):
        wait_received(*grad_args(q))
        add_state(q, returned, main, fifth, inverse, total, state, out, leave_state)
        wait_sent(*grad_args(q))
    wait_received(*own_args)
    all_station_scores(gathered, scores_out)
    leave[1].start()
    wait_sent(*own_args)
    for copy in leave:
        copy.wait()
    for copy in leave_state:
        copy.wait()


def hand_over(*refs):
    count = len(refs) // 2
    for i in range(count):
        refs[count + i][...] = refs[i][...]


def shards(ensemble, mix_weight, analysis, station_weight, station_obs, block_band, block_start):
    smem = pl.BlockSpec(memory_space=pltpu.SMEM)
    vmem = pl.BlockSpec(memory_space=pltpu.VMEM)
    anywhere = pl.BlockSpec(memory_space=pl.ANY)
    message = (CHUNKS, MEMBERS, 16, PIECE)
    sems = pltpu.SemaphoreType.DMA((2,))
    piece_sems = pltpu.SemaphoreType.DMA((CHUNKS, 2))
    shapes = (
        jax.ShapeDtypeStruct((5, ROWS, LON), F32),
        jax.ShapeDtypeStruct((16, STATIONS, FIELDS), F32),
        jax.ShapeDtypeStruct((1, ROWS, FIELDS, LON), BF),
    )
    outs = pl.pallas_call(
        kernel,
        out_shape=tuple(pltpu.VMEM(shape.shape, shape.dtype) for shape in shapes),
        in_specs=[smem] * 3 + [anywhere, vmem] + [anywhere] * 4,
        out_specs=(anywhere,) * 3,
        scratch_shapes=[
            pltpu.SMEM((SLOTS,), jnp.int32),
            pltpu.SMEM((16,), jnp.int32),
            pltpu.VMEM((1, ROWS, FIELDS, LON), BF),
            pltpu.VMEM((16, STATIONS * ROWS, 128), BF),
            pltpu.VMEM((16, STATIONS, FIELDS), BF),
            pltpu.VMEM((5, ROWS, LON), BF),
            pltpu.VMEM((LAYERS + 1, EXT, FIELDS, LANES), BF),
            pltpu.VMEM((LANES, LANES), BF),
            pltpu.VMEM((BANDS, 16, 128), BF),
            pltpu.VMEM((BANDS, 16, 128), BF),
            pltpu.VMEM((BANDS // 2, 16, 128), BF),
            pltpu.VMEM((16, 64, 128), BF),
            pltpu.VMEM((BANDS, 128, 128), BF),
            pltpu.VMEM((BANDS, 128, 128), BF),
            pltpu.VMEM((BANDS, 16, 128), BF),
            pltpu.VMEM((BANDS, 16, 128), BF),
            pltpu.VMEM((MEMBERS, BANDS // 2, 16, 128), BF),
            pltpu.VMEM((ROWS, POINTS, LANES), BF),
            pltpu.VMEM(message, BF),
            pltpu.VMEM(message, BF),
            pltpu.VMEM(message, BF),
            pltpu.VMEM(message, BF),
            pltpu.VMEM((512, LANES), BF),
            pltpu.VMEM((128, POINTS), F32),
            pltpu.VMEM((128, POINTS), BF),
            pltpu.VMEM(message, F32),
            pltpu.VMEM((512, CHUNK), BF),
            pltpu.VMEM((CHUNKS, 16, PIECE), F32),
            pltpu.VMEM((8, POINTS), F32),
            pltpu.VMEM((CHUNKS, 16, PIECE), F32),
            pltpu.VMEM((BANDS, 8, 128), F32),
            pltpu.VMEM((BANDS, 8, 128), F32),
            pltpu.VMEM((16, 256), BF),
            pltpu.VMEM((MEMBERS, 16, 256), BF),
            pltpu.VMEM((ROWS * FIELDS, CHUNK), BF),
            pltpu.VMEM((ROWS * FIELDS, LON), F32),
            pltpu.VMEM((5, ROWS, LON), F32),
            pltpu.VMEM((16, STATIONS, FIELDS), F32),
            pltpu.VMEM((1, ROWS, FIELDS, LON), BF),
            pltpu.SemaphoreType.DMA((ROWS + 4,)),
            pltpu.SemaphoreType.DMA((2 + CHUNKS,)),
            pltpu.SemaphoreType.DMA((2 * HALO, 2)),
            sems, sems, sems, sems, piece_sems, sems, sems, piece_sems,
        ],
        compiler_params=pltpu.CompilerParams(
            vmem_limit_bytes=56 * MIB, collective_id=0, has_side_effects=True
        ),
    )(
        block_band.reshape(-1), block_start, jnp.asarray(row_factors()), ensemble, mix_weight,
        station_weight.reshape(16, STATIONS * ROWS, 128),        station_obs, jnp.transpose(analysis, (1, 0, 2)), jnp.asarray(inverse_table()),
    )
    score, station, state = pl.pallas_call(
        hand_over,
        out_shape=shapes,
        in_specs=[vmem] * 3,
        out_specs=(vmem,) * 3,
        compiler_params=pltpu.CompilerParams(vmem_limit_bytes=16 * MIB),
    )(*outs)
    return jnp.transpose(score, (1, 0, 2)), station, state


def solution(mesh):
    return jax.shard_map(
        shards,
        mesh=mesh,
        in_specs=(
            P("member", "band", None, None),
            P(),
            P("band", "member", None),
            P("band", None, None, None),
            P("band", None, None),
            P(),
            P(),
        ),
        out_specs=(
            P("band", "member", None),
            P("band", None, None),
            P("member", "band", None, None),
        ),
        check_vma=False,
    )
```

```python
import math

import jax
import jax.numpy as jnp
import numpy as np
from jax import lax
from jax.experimental import pallas as pl
from jax.experimental.pallas import tpu as pltpu
from jax.sharding import PartitionSpec as P

CAP = 2
DIFFUSION = 4.0

ROWS = 4
HALO = 3
EXT = ROWS + 2 * HALO
FIELDS = 80
LON = 1440
LANES = 1536
CHUNKS = 3
CHUNK = LANES // CHUNKS
TILES = CHUNK // 128
PIECE = CHUNK + 128
MEMBERS = 16
BANDS = 16
TOTAL_ROWS = 64
LAYERS = 3
SLOTS = BANDS * CAP
STATIONS = 32
POINTS = SLOTS * STATIONS
PAIRS = MEMBERS * (MEMBERS - 1) // 2
MIB = 1 << 20

BF = jnp.bfloat16
F32 = jnp.float32


def inverse_table():
    centre = 1.0 + 2.0 * DIFFUSION
    root = (centre - math.sqrt(centre * centre - 4.0 * DIFFUSION * DIFFUSION)) / (2.0 * DIFFUSION)
    factor = 1.0 / (DIFFUSION * (1.0 / root - root) * (1.0 - root**LON))
    offset = np.abs(np.arange(LON)[:, None] - np.arange(LON)[None, :])
    nearest = np.minimum(offset, LON - offset).astype(np.float64)
    values = (np.exp(nearest * math.log(root)) + np.exp((LON - nearest) * math.log(root))) * factor
    table = np.zeros((LANES, LANES), np.float32)
    table[:LON, :LON] = values
    return table.astype(BF)


def row_factors():
    rows = np.arange(-HALO, TOTAL_ROWS + HALO)
    cosine = np.cos(math.pi * ((rows + 0.5) / TOTAL_ROWS - 0.5))
    metric = 1.0 / (cosine * cosine + 0.1)
    inside = (rows >= 0) & (rows < TOTAL_ROWS)
    return np.stack([metric / (2 + 2 * metric), 1 / (2 + 2 * metric), inside], axis=1).astype(np.float32)


def hot(condition):
    return jnp.where(condition, 1.0, 0.0).astype(BF)


def iota(shape, dim):
    return lax.broadcasted_iota(jnp.int32, shape, dim)


def grid_to_message(transposed):
    shape = (320, 256) if transposed else (256, 320)
    row, col = iota(shape, int(transposed)), iota(shape, 1 - int(transposed))
    group, place = row >> 4, row & 15
    main = hot(col == (place >> 2) * FIELDS + group * 5 + (place & 3))
    fifth = col == (place & 3) * FIELDS + group * 5 + 4
    return main, [hot(fifth & ((place >> 2) == t)) for t in range(TILES)]


def message_to_station(transposed):
    shape = (256, 512) if transposed else (512, 256)
    row, col = iota(shape, int(transposed)), iota(shape, 1 - int(transposed))
    r, member, f = row >> 7, (row >> 3) & 15, row & 7
    same = member == (col >> 4)
    place = col & 15
    main = hot(same & (f < 4) & (place == r * 4 + f))
    return main, [hot(same & (f == 4) & (place == t * 4 + r)) for t in range(TILES)]


def lane_tile(t):
    return slice(t * 128, (t + 1) * 128)


def lane_chunk(q):
    return slice(q * CHUNK, (q + 1) * CHUNK)


def dot(a, b):
    return jnp.dot(a, b, preferred_element_type=F32)


def dot_t(a, b):
    return lax.dot_general(a, b, (((1,), (1,)), ((), ())), preferred_element_type=F32)


def stencil_row(u, nxt, weight, row, east_west, north_south, inside):
    tiles = LANES // 128
    lane = iota((FIELDS, 128), 1)

    def tile(at, t):
        return u[at, :, t * 128 : (t + 1) * 128].astype(F32)

    first, last = tile(row, 0), tile(row, tiles - 1)
    wrapped = jnp.where(lane == LON % 128, pltpu.roll(first, LON % 128, 1), last)
    before = pltpu.roll(last, 129 - LON % 128, 1)
    here = first
    ahead = pltpu.roll(here, 127, 1)
    for pair in range(tiles // 2):
        values, middles = [], []
        for t in (2 * pair, 2 * pair + 1):
            after = wrapped if t == tiles - 2 else (tile(row, t + 1) if t < tiles - 1 else here)
            further = pltpu.roll(after, 127, 1) if t < tiles - 1 else ahead
            east = jnp.where(lane == 127, further, ahead)
            moved = pltpu.roll(here, 1, 1)
            west = jnp.where(lane == 0, before, moved)
            sides = tile(row - 1, t) + tile(row + 1, t)
            values.append((east + west) * east_west + sides * north_south - here)
            middles.append(here)
            before, here, ahead = moved, after, further
        mixed = dot(weight, jnp.concatenate(values, axis=1).astype(BF))
        fresh = jnp.concatenate(middles, axis=1) + jnp.tanh(mixed)
        if inside is not None:
            fresh = fresh * inside
        nxt[row, :, pair * 256 : (pair + 1) * 256] = fresh.astype(BF)


def diffuse_chunk(q, rows, inverse, main, fifth, message):
    piece = dot(rows, inverse[:, lane_chunk(q)]).astype(BF)
    message[q, :, :, :CHUNK] = dot(main, piece).astype(BF).reshape(MEMBERS, 16, CHUNK)
    below = sum(dot(fifth[t], piece[:, lane_tile(t)]) for t in range(TILES))
    message[q, :, :, CHUNK:] = below.astype(BF).reshape(MEMBERS, 16, 128)


def pair_terms(values, truth):
    slopes = [None] * MEMBERS
    total = None
    for i in range(MEMBERS):
        for j in range(i + 1, MEMBERS):
            spread = values[i] - values[j]
            square = spread * spread + 1.0
            inverse = lax.rsqrt(square)
            slope = spread * inverse
            root = square * inverse
            total = root if total is None else total + root
            slopes[i] = slope if slopes[i] is None else slopes[i] + slope
            slopes[j] = -slope if slopes[j] is None else slopes[j] - slope
    error_total = None
    grads = []
    for m in range(MEMBERS):
        error = values[m] - truth
        square = error * error + 1.0
        inverse = lax.rsqrt(square)
        root = square * inverse
        error_total = root if error_total is None else error_total + root
        grads.append(error * inverse - slopes[m] * (1.0 / (MEMBERS - 1)))
    score = (error_total - MEMBERS) * (1.0 / MEMBERS) - (total - PAIRS) * (1.0 / (MEMBERS * (MEMBERS - 1)))
    return score, grads


def send(src, dst, sems, device):
    return pltpu.make_async_remote_copy(
        src_ref=src,
        dst_ref=dst,
        send_sem=sems.at[0],
        recv_sem=sems.at[1],
        device_id=device,
        device_id_type=pl.DeviceIdType.MESH,
    )


def member_at(member, step, sign):
    x = (member + sign * (step & 3)) & 3
    y = ((member >> 2) + sign * (step >> 2)) & 3
    return y * 4 + x


def band_at(band, step, sign):
    return (band + sign * step) & (BANDS - 1)


def exchange(source, target, sems, me, at, axis):
    @pl.loop(1, 16)
    def _(step):
        peer = at(me, step, 1)
        send(source(peer), target.at[me], sems, {axis: peer}).start()


def all_others(target, sems, me, at, axis):
    whole = target.at[0:15]
    return send(whole, whole, sems, {axis: at(me, 1, 1)})


def wait_received(source, target, sems, me, at, axis):
    all_others(target, sems, me, at, axis).wait_recv()


def wait_sent(source, target, sems, me, at, axis):
    all_others(target, sems, me, at, axis).wait_send()


def find_slots(band_ref, band, slot_ref):
    own = [band_ref[band * 16 + k] for k in range(16)]
    for k in range(16):
        rank = jnp.int32(0)
        for i in range(k):
            rank += jnp.where(own[i] == own[k], 1, 0)
        slot_ref[k] = own[k] * CAP + rank


def find_starts(band_ref, first_ref, band, start_ref):
    @pl.loop(0, BANDS)
    def _(home):
        seen, first, second = jnp.int32(0), jnp.int32(0), jnp.int32(0)
        for k in range(16):
            match = band_ref[home * 16 + k] == band
            here = first_ref[home * 16 + k]
            first = jnp.where(match & (seen == 0), here, first)
            second = jnp.where(match & (seen == 1), here, second)
            seen += jnp.where(match, 1, 0)
        start_ref[home * CAP] = first
        start_ref[home * CAP + 1] = second


def outgoing_shares(slot_ref, weight_ref, member, zout):
    row, col = iota((8, 128), 0), iota((8, 128), 1)
    own = hot(col == (16 + (member & 1) * 8 + row) * ROWS + ((member >> 1) & 3))
    share = jnp.concatenate([dot(own, weight_ref[k]) for k in range(16)], axis=0).astype(BF)
    lane = iota((1, 128), 1)
    slot_row = jnp.zeros((1, 128), jnp.int32)
    for k in range(16):
        slot_row = jnp.where((lane >> 3) == k, slot_ref[k], slot_row)
    row, col = iota((128, 128), 0), iota((128, 128), 1)
    pick = hot(((row >> 3) * CAP + (member >> 3) == slot_row) & ((row & 7) == (col & 7)))
    picked = dot(pick, share)
    for b in range(BANDS):
        zout[b] = jnp.concatenate([picked[b * 8 : b * 8 + 8], jnp.zeros((8, 128), F32)], axis=0).astype(BF)


def join_shares(zin, joined):
    for pair in range(BANDS // 2):
        parts = [zin[2 * pair + odd].astype(F32)[0:8] for odd in range(2)]
        joined[pair] = jnp.concatenate(parts, axis=0).astype(BF)


def outgoing_direct(slot_ref, weight_ref, turned, direct_out):
    row, col = iota((64, 128), 0), iota((64, 128), 1)
    pick = hot(col == (row & 15) * ROWS + (row >> 4))
    for k in range(16):
        turned[k] = dot(pick, weight_ref[k]).astype(BF)

    @pl.loop(0, BANDS)
    def _(b):
        for cap in range(CAP):
            block = jnp.zeros((64, 128), BF)
            for k in range(16):
                block = jnp.where(jnp.full((64, 128), slot_ref[k], jnp.int32) == b * CAP + cap, turned[k], block)
            direct_out[b, cap * 64 : (cap + 1) * 64, :] = block


def outgoing_obs(slot_ref, obs_ref, member, obs_out):
    row, col = iota((16, FIELDS), 0), iota((16, FIELDS), 1)
    pick = hot((row < 5) & (col == member * 5 + row))
    own = dot_t(pick, obs_ref[...].reshape(16 * STATIONS, FIELDS))[0:8]
    group = iota((8, 128), 1) >> 5
    blocks = []
    for k in range(16):
        block = jnp.where(group == (k & 3), own[:, lane_tile(k >> 2)], 0.0)
        block += pltpu.roll(block, 32, 1)
        blocks.append(block + pltpu.roll(block, 64, 1))
    for t in range(SLOTS // 4):
        tile = jnp.zeros((8, 128), F32)
        for k in range(16):
            tile = jnp.where(group + 4 * t == slot_ref[k], blocks[k], tile)
        for odd in range(2):
            piece = pltpu.roll(tile, 64, 1) if odd else tile
            obs_out[2 * t + odd] = jnp.concatenate([piece, jnp.zeros((8, 128), F32)], axis=0).astype(BF)


def spread_out_weights(start_ref, direct, weights, spread_weight):
    lane = iota((STATIONS, 128), 1)

    @pl.loop(0, BANDS // 2)
    def _(pair):
        for cap in range(CAP):
            shares = [
                [weights[cap * 8 + r * 2 + g, pair].astype(F32) for g in range(2)] for r in range(ROWS)
            ]
            for odd in range(2):
                home = pair * 2 + odd
                start = start_ref[home * CAP + cap]
                shift = start & 127
                at = pl.ds(home * 64 + cap * STATIONS, STATIONS)
                moved = []
                for r in range(ROWS):
                    near = direct[home, cap * 64 + r * 16 : cap * 64 + r * 16 + 16, :].astype(F32)
                    passed = [share[odd * 8 : odd * 8 + 8] for share in shares[r]]
                    moved.append(pltpu.roll(jnp.concatenate([near] + passed, axis=0), shift, 1))
                for t in range(LANES // 128):
                    place = lane + t * 128 - start
                    inside = (place >= 0) & (place < 128)
                    for r in range(ROWS):
                        spread_weight[r, at, lane_tile(t)] = jnp.where(inside, moved[r], 0.0).astype(BF)


def fold_truth(truth_ref, truth):
    truth[...] = jnp.zeros((CHUNKS, 16, PIECE), F32)
    fields = [truth_ref[f].astype(F32) for f in range(5)]
    for q in range(CHUNKS):
        width = min(CHUNK, LON - q * CHUNK)
        for r in range(ROWS):
            for f in range(4):
                truth[q, 4 * r + f : 4 * r + f + 1, :width] = fields[f][r : r + 1, q * CHUNK : q * CHUNK + width]
        for t in range(TILES):
            first = q * CHUNK + t * 128
            width = min(128, LON - first)
            truth[q, 4 * t : 4 * t + 4, CHUNK : CHUNK + width] = fields[4][:, first : first + width]


def unfold_score(score, score_ref):
    for q in range(CHUNKS):
        width = min(CHUNK, LON - q * CHUNK)
        for r in range(ROWS):
            for f in range(4):
                score_ref[f, r : r + 1, q * CHUNK : q * CHUNK + width] = score[
                    q, 4 * r + f : 4 * r + f + 1, :width
                ]
        for t in range(TILES):
            first = q * CHUNK + t * 128
            width = min(128, LON - first)
            score_ref[4, :, first : first + width] = score[q, 4 * t : 4 * t + 4, CHUNK : CHUNK + width]


def join_obs(obs_in, obs):
    lane = iota((8, 128), 1)
    for t in range(POINTS // 128):
        low = obs_in[2 * t].astype(F32)[0:8]
        high = obs_in[2 * t + 1].astype(F32)[0:8]
        obs[:, lane_tile(t)] = jnp.where(lane < 64, low, pltpu.roll(high, 64, 1))


def station_rows(q, received, main, fifth, rows):
    for t in range(TILES):
        tile = dot(main, received[q, :, :, lane_tile(t)].reshape(256, 128))
        tile += dot(fifth[t], received[q, :, :, CHUNK:].reshape(256, 128))
        rows[:, lane_tile(q * TILES + t)] = tile.astype(BF)


def estimates(first, stop, rows, spread_weight, est):
    for r in range(ROWS):
        part = dot_t(rows[r * 128 : (r + 1) * 128, first:stop], spread_weight[r, :, first:stop])
        est[...] = part if r == 0 and first == 0 else est[...] + part


def station_scores(est, slopes, obs, station_out):
    lane = iota((8, 128), 1)

    @pl.loop(0, POINTS // 256)
    def _(n):
        for half in range(2):
            at = pl.ds(pl.multiple_of(n * 256 + half * 128, 128), 128)
            members = [est[m * 8 : (m + 1) * 8, at] for m in range(MEMBERS)]
            total, grads = pair_terms(members, obs[:, at])
            other = pltpu.roll(total, 64, 1)
            station_out[4 * n + 2 * half] = jnp.where(lane < 64, total, other)
            station_out[4 * n + 2 * half + 1] = jnp.where(lane < 64, other, total)
            for m in range(0, MEMBERS, 2):
                slopes[m * 8 : m * 8 + 16, at] = jnp.concatenate(grads[m : m + 2], axis=0).astype(BF)


def grid_pairs(q, received, values, truth, score):
    values[q] = received[q].astype(F32)

    @pl.loop(0, PIECE // 128)
    def _(n):
        at = pl.ds(pl.multiple_of(n * 128, 128), 128)
        for half in range(2):
            part = slice(half * 8, half * 8 + 8)
            members = [values[q, m, part, at] for m in range(MEMBERS)]
            total, grads = pair_terms(members, truth[q, part, at])
            score[q, part, at] = total
            for m in range(MEMBERS):
                values[q, m, part, at] = grads[m]


def spread_chunk(q, slopes, spread_weight, spread):
    for r in range(ROWS):
        part = dot(slopes[...], spread_weight[r, :, lane_chunk(q)])
        spread[r * 128 : (r + 1) * 128, :] = part.astype(BF)


def total_chunk(q, values, spread, back, back_fifth, grad):
    total = values[q, :, :, :CHUNK].reshape(256, CHUNK) + dot(back, spread[...])
    grad[q, :, :, :CHUNK] = total.astype(BF).reshape(MEMBERS, 16, CHUNK)
    below = values[q, :, :, CHUNK:].reshape(256, 128)
    for t in range(TILES):
        below += dot(back_fifth[t], spread[:, lane_tile(t)])
    grad[q, :, :, CHUNK:] = below.astype(BF).reshape(MEMBERS, 16, 128)


def own_station_scores(slot_ref, station_in, own):
    group = iota((8, 128), 1) >> 5
    even = (group & 1) == 0
    pieces = []
    for b in range(BANDS):
        here = station_in[b]
        moved = pltpu.roll(here, 32, 1)
        pieces.append(jnp.where(even, here, moved))
        pieces.append(jnp.where(even, moved, here))
    tiles = []
    for t in range(4):
        slot = jnp.zeros((8, 128), jnp.int32)
        for g in range(4):
            slot = jnp.where(group == g, slot_ref[4 * t + g], slot)
        tile = jnp.zeros((8, 128), F32)
        for at in range(SLOTS):
            tile = jnp.where(slot == at, pieces[at], tile)
        tiles.append(tile)
    for t in range(2):
        own[:, lane_tile(t)] = jnp.concatenate([tiles[t], tiles[t + 2]], axis=0).astype(BF)


def all_station_scores(gathered, station_ref):
    row, col = iota((256, FIELDS), 0), iota((256, FIELDS), 1)
    field = (row >> 4) * 5 + (row & 7)
    whole = gathered[...].reshape(256, 256)
    dims = (((0,), (0,)), ((), ()))
    for half in range(2):
        pick = hot(((row & 7) < 5) & (field == col) & (((row >> 3) & 1) == half))
        joined = lax.dot_general(whole, pick, dims, preferred_element_type=F32)
        station_ref[half * 8 : half * 8 + 8] = joined.reshape(8, STATIONS, FIELDS)


def add_state(q, returned, main, fifth, inverse, total, state, out, copies):
    for t in range(TILES):
        tile = dot(main, returned[q, :, :, lane_tile(t)].reshape(256, 128))
        tile += dot(fifth[t], returned[q, :, :, CHUNK:].reshape(256, 128))
        total[:, lane_tile(t)] = tile.astype(BF)
    for n in range(CHUNKS):
        width = min(CHUNK, LON - n * CHUNK)
        at = slice(n * CHUNK, n * CHUNK + width)
        part = dot(total[...], inverse[lane_chunk(q), at])
        if q > 0:
            part += state[:, at]
        if q < CHUNKS - 1:
            state[:, at] = part
        else:
            out[0, :, :, at] = part.astype(BF).reshape(ROWS, FIELDS, width)
            copies[n].start()


def kernel(
    band_ref, first_ref, factor_ref, state_hbm, mix_ref, weight_hbm, obs_hbm, truth_hbm, inverse_hbm,
    score_ref, station_ref, out_ref,
    start_ref, slot_ref,
    state_ref, weight_ref, obs_ref, truth_ref,
    layers, inverse, zout, zin, joined, turned, direct_out, direct_in, obs_out, obs_in, weights, spread_weight, message, received, grad, returned,
    rows, est, slopes, values, spread, truth, obs, score, station_out, station_in, own, gathered,
    total, state, score_out, scores_out, out,
    fetch_sem, leave_sem, halo_sem, z_sem, obs_sem, direct_sem, weight_sem, message_sem, station_sem, own_sem, grad_sem,
):
    band = lax.axis_index("band")
    member = lax.axis_index("member")
    barrier = pltpu.get_barrier_semaphore()

    @pl.loop(1, 16)
    def _(step):
        for device in ({"member": member_at(member, step, 1)}, {"band": band_at(band, step, 1)}):
            pl.semaphore_signal(barrier, inc=1, device_id=device, device_id_type=pl.DeviceIdType.MESH)

    fetches = [
        pltpu.make_async_copy(source, target, fetch_sem.at[i])
        for i, (source, target) in enumerate(
            [(state_hbm.at[0, r], state_ref.at[0, r]) for r in range(ROWS)]
            + [
                (weight_hbm, weight_ref), (obs_hbm, obs_ref), (truth_hbm, truth_ref),
                (inverse_hbm, inverse),
            ]
        )
    ]
    for fetch in fetches:
        fetch.start()

    u = layers.at[0]
    u[HALO : HALO + ROWS, :, LON - 32 :] = jnp.zeros((ROWS, FIELDS, LANES - LON + 32), BF)

    @pl.when(band == 0)
    def _():
        u[0:HALO] = jnp.zeros((HALO, FIELDS, LANES), BF)

    @pl.when(band == BANDS - 1)
    def _():
        u[HALO + ROWS :] = jnp.zeros((HALO, FIELDS, LANES), BF)

    find_slots(band_ref, band, slot_ref)
    for fetch in fetches[:ROWS]:
        fetch.wait()
    u[HALO : HALO + ROWS, :, :LON] = state_ref[0]

    def to_north(i):
        return send(u.at[HALO + ROWS - 1 - i], u.at[HALO - 1 - i], halo_sem.at[i], {"band": band_at(band, 1, 1)})

    def to_south(i):
        return send(u.at[HALO + i], u.at[HALO + ROWS + i], halo_sem.at[HALO + i], {"band": band_at(band, 1, -1)})

    def send_halo(i):
        pl.when(band < BANDS - 1)(to_north(i).start)
        pl.when(band > 0)(to_south(i).start)

    direct_args = (lambda b: direct_out.at[b], direct_in, direct_sem, band, band_at, "band")
    weight_args = (lambda m: joined, weights, weight_sem, member, member_at, "member")
    z_args = (lambda b: zout.at[b], zin, z_sem, band, band_at, "band")
    obs_args = (lambda b: obs_out.at[b], obs_in, obs_sem, band, band_at, "band")
    station_args = (lambda b: station_out.at[b], station_in, station_sem, band, band_at, "band")
    own_args = (lambda m: own, gathered, own_sem, member, member_at, "member")

    def message_args(q):
        return lambda m: message.at[q, m], received.at[q], message_sem.at[q], member, member_at, "member"

    def grad_args(q):
        return lambda m: grad.at[q, m], returned.at[q], grad_sem.at[q], member, member_at, "member"

    core = band & 1

    def run(*steps):
        for layer, place in steps:
            row = place + core * (EXT - 1 - 2 * place)
            factor = band * ROWS + row
            own = HALO <= place < HALO + ROWS
            stencil_row(
                layers.at[layer], layers.at[layer + 1], mix_ref[layer], row,
                factor_ref[factor, 0], factor_ref[factor, 1], None if own else factor_ref[factor, 2],
            )

    def wait_near(i):
        pl.when(core == 1)(to_north(i).wait_recv)
        pl.when(core == 0)(to_south(i).wait_recv)

    def wait_far(i):
        pl.when((core == 0) & (band > 0))(to_north(i).wait_recv)
        pl.when((core == 1) & (band < BANDS - 1))(to_south(i).wait_recv)

    run((0, 4), (0, 5))
    fetches[ROWS].wait()
    outgoing_shares(slot_ref, weight_ref, member, zout)
    fetches[ROWS + 1].wait()
    outgoing_obs(slot_ref, obs_ref, member, obs_out)
    outgoing_direct(slot_ref, weight_ref, turned, direct_out)
    pl.semaphore_wait(barrier, 30)
    send_halo(0)
    exchange(*z_args)
    send_halo(1)
    send_halo(2)
    zin[band] = zout[band]
    obs_in[band] = obs_out[band]
    direct_in[band] = direct_out[band]
    find_starts(band_ref, first_ref, band, start_ref)
    fetches[ROWS + 2].wait()
    fold_truth(truth_ref, truth)
    for i in range(HALO):
        wait_near(i)
    run((0, 6), (0, 7))
    run((1, 5), (0, 8))
    run((1, 6), (1, 7))
    run((2, 6))
    wait_far(0)
    run((0, 3), (1, 4), (2, 5))
    wait_received(*z_args)
    join_shares(zin, joined)
    exchange(*weight_args)
    weights[member] = joined[...]
    wait_far(1)
    run((0, 2), (1, 3), (2, 4))
    wait_far(2)
    exchange(*obs_args)
    exchange(*direct_args)
    run((0, 1), (1, 2), (2, 3))

    fetches[ROWS + 3].wait()
    main, fifth = grid_to_message(False)
    grid_rows = layers[LAYERS, HALO : HALO + ROWS].reshape(ROWS * FIELDS, LANES)
    for q in range(CHUNKS):
        diffuse_chunk(q, grid_rows, inverse, main, fifth, message)
        exchange(*message_args(q))
        received[q, member] = message[q, member]

    main, fifth = message_to_station(False)
    for q in range(CHUNKS - 1):
        wait_received(*message_args(q))
        station_rows(q, received, main, fifth, rows)
        if q == 0:
            grid_pairs(q, received, values, truth, score)
        else:
            wait_received(*obs_args)
            join_obs(obs_in, obs)
            wait_received(*weight_args)
            wait_received(*direct_args)
            spread_out_weights(start_ref, direct_in, weights, spread_weight)

    estimates(0, CHUNK * (CHUNKS - 1), rows, spread_weight, est)
    wait_received(*message_args(CHUNKS - 1))
    station_rows(CHUNKS - 1, received, main, fifth, rows)
    estimates(CHUNK * (CHUNKS - 1), LANES, rows, spread_weight, est)
    station_scores(est, slopes, obs, station_out)
    def share_station_scores():
        wait_received(*station_args)
        own_station_scores(slot_ref, station_in, own)
        exchange(*own_args)
        gathered[member] = own[...]

    back, back_fifth = message_to_station(True)
    for q in range(CHUNKS):
        spread_chunk(q, slopes, spread_weight, spread)
        if q > 0:
            grid_pairs(q, received, values, truth, score)
        total_chunk(q, values, spread, back, back_fifth, grad)
        exchange(*grad_args(q))
        if q == 0:
            exchange(*station_args)
            station_in[band] = station_out[band]
        returned[q, member] = grad[q, member]

    leave = [
        pltpu.make_async_copy(score_out, score_ref, leave_sem.at[0]),
        pltpu.make_async_copy(scores_out, station_ref, leave_sem.at[1]),
    ]
    leave_state = []
    for n in range(CHUNKS):
        at = slice(n * CHUNK, min((n + 1) * CHUNK, LON))
        leave_state.append(pltpu.make_async_copy(out.at[:, :, :, at], out_ref.at[:, :, :, at], leave_sem.at[2 + n]))
    unfold_score(score, score_out)
    leave[0].start()
    share_station_scores()
    for i in range(HALO):
        pl.when(band < BANDS - 1)(to_north(i).wait_send)
        pl.when(band > 0)(to_south(i).wait_send)
    for args in (obs_args, z_args, direct_args, weight_args, station_args):
        wait_sent(*args)
    for q in range(CHUNKS):
        wait_sent(*message_args(q))

    main, fifth = grid_to_message(True)
    for q in range(CHUNKS):
        wait_received(*grad_args(q))
        add_state(q, returned, main, fifth, inverse, total, state, out, leave_state)
        wait_sent(*grad_args(q))
    wait_received(*own_args)
    all_station_scores(gathered, scores_out)
    leave[1].start()
    wait_sent(*own_args)
    for copy in leave:
        copy.wait()
    for copy in leave_state:
        copy.wait()


def hand_over(*refs):
    count = len(refs) // 2
    for i in range(count):
        refs[count + i][...] = refs[i][...]


def shards(ensemble, mix_weight, analysis, station_weight, station_obs, block_band, block_start):
    smem = pl.BlockSpec(memory_space=pltpu.SMEM)
    vmem = pl.BlockSpec(memory_space=pltpu.VMEM)
    anywhere = pl.BlockSpec(memory_space=pl.ANY)
    message = (CHUNKS, MEMBERS, 16, PIECE)
    sems = pltpu.SemaphoreType.DMA((2,))
    piece_sems = pltpu.SemaphoreType.DMA((CHUNKS, 2))
    shapes = (
        jax.ShapeDtypeStruct((5, ROWS, LON), F32),
        jax.ShapeDtypeStruct((16, STATIONS, FIELDS), F32),
        jax.ShapeDtypeStruct((1, ROWS, FIELDS, LON), BF),
    )
    outs = pl.pallas_call(
        kernel,
        out_shape=tuple(pltpu.VMEM(shape.shape, shape.dtype) for shape in shapes),
        in_specs=[smem] * 3 + [anywhere, vmem] + [anywhere] * 4,
        out_specs=(anywhere,) * 3,
        scratch_shapes=[
            pltpu.SMEM((SLOTS,), jnp.int32),
            pltpu.SMEM((16,), jnp.int32),
            pltpu.VMEM((1, ROWS, FIELDS, LON), BF),
            pltpu.VMEM((16, STATIONS * ROWS, 128), BF),
            pltpu.VMEM((16, STATIONS, FIELDS), BF),
            pltpu.VMEM((5, ROWS, LON), BF),
            pltpu.VMEM((LAYERS + 1, EXT, FIELDS, LANES), BF),
            pltpu.VMEM((LANES, LANES), BF),
            pltpu.VMEM((BANDS, 16, 128), BF),
            pltpu.VMEM((BANDS, 16, 128), BF),
            pltpu.VMEM((BANDS // 2, 16, 128), BF),
            pltpu.VMEM((16, 64, 128), BF),
            pltpu.VMEM((BANDS, 128, 128), BF),
            pltpu.VMEM((BANDS, 128, 128), BF),
            pltpu.VMEM((BANDS, 16, 128), BF),
            pltpu.VMEM((BANDS, 16, 128), BF),
            pltpu.VMEM((MEMBERS, BANDS // 2, 16, 128), BF),
            pltpu.VMEM((ROWS, POINTS, LANES), BF),
            pltpu.VMEM(message, BF),
            pltpu.VMEM(message, BF),
            pltpu.VMEM(message, BF),
            pltpu.VMEM(message, BF),
            pltpu.VMEM((512, LANES), BF),
            pltpu.VMEM((128, POINTS), F32),
            pltpu.VMEM((128, POINTS), BF),
            pltpu.VMEM(message, F32),
            pltpu.VMEM((512, CHUNK), BF),
            pltpu.VMEM((CHUNKS, 16, PIECE), F32),
            pltpu.VMEM((8, POINTS), F32),
            pltpu.VMEM((CHUNKS, 16, PIECE), F32),
            pltpu.VMEM((BANDS, 8, 128), F32),
            pltpu.VMEM((BANDS, 8, 128), F32),
            pltpu.VMEM((16, 256), BF),
            pltpu.VMEM((MEMBERS, 16, 256), BF),
            pltpu.VMEM((ROWS * FIELDS, CHUNK), BF),
            pltpu.VMEM((ROWS * FIELDS, LON), F32),
            pltpu.VMEM((5, ROWS, LON), F32),
            pltpu.VMEM((16, STATIONS, FIELDS), F32),
            pltpu.VMEM((1, ROWS, FIELDS, LON), BF),
            pltpu.SemaphoreType.DMA((ROWS + 4,)),
            pltpu.SemaphoreType.DMA((2 + CHUNKS,)),
            pltpu.SemaphoreType.DMA((2 * HALO, 2)),
            sems, sems, sems, sems, piece_sems, sems, sems, piece_sems,
        ],
        compiler_params=pltpu.CompilerParams(
            vmem_limit_bytes=56 * MIB, collective_id=0, has_side_effects=True
        ),
    )(
        block_band.reshape(-1), block_start, jnp.asarray(row_factors()), ensemble, mix_weight,
        station_weight.reshape(16, STATIONS * ROWS, 128),        station_obs, jnp.transpose(analysis, (1, 0, 2)), jnp.asarray(inverse_table()),
    )
    score, station, state = pl.pallas_call(
        hand_over,
        out_shape=shapes,
        in_specs=[vmem] * 3,
        out_specs=(vmem,) * 3,
        compiler_params=pltpu.CompilerParams(vmem_limit_bytes=16 * MIB),
    )(*outs)
    return jnp.transpose(score, (1, 0, 2)), station, state


def solution(mesh):
    return jax.shard_map(
        shards,
        mesh=mesh,
        in_specs=(
            P("member", "band", None, None),
            P(),
            P("band", "member", None),
            P("band", None, None, None),
            P("band", None, None),
            P(),
            P(),
        ),
        out_specs=(
            P("band", "member", None),
            P("band", None, None),
            P("member", "band", None, None),
        ),
        check_vma=False,
    )
```

```python
import math

import jax
import jax.numpy as jnp
import numpy as np
from jax import lax
from jax.experimental import pallas as pl
from jax.experimental.pallas import tpu as pltpu
from jax.sharding import PartitionSpec as P

CAP = 2
DIFFUSION = 4.0

ROWS = 4
HALO = 3
EXT = ROWS + 2 * HALO
FIELDS = 80
LON = 1440
LANES = 1536
CHUNKS = 3
CHUNK = LANES // CHUNKS
TILES = CHUNK // 128
PIECE = CHUNK + 128
MEMBERS = 16
BANDS = 16
TOTAL_ROWS = 64
LAYERS = 3
SLOTS = BANDS * CAP
STATIONS = 32
POINTS = SLOTS * STATIONS
PAIRS = MEMBERS * (MEMBERS - 1) // 2
MIB = 1 << 20

BF = jnp.bfloat16
F32 = jnp.float32


def inverse_table():
    centre = 1.0 + 2.0 * DIFFUSION
    root = (centre - math.sqrt(centre * centre - 4.0 * DIFFUSION * DIFFUSION)) / (2.0 * DIFFUSION)
    factor = 1.0 / (DIFFUSION * (1.0 / root - root) * (1.0 - root**LON))
    offset = np.abs(np.arange(LON)[:, None] - np.arange(LON)[None, :])
    nearest = np.minimum(offset, LON - offset).astype(np.float64)
    values = (np.exp(nearest * math.log(root)) + np.exp((LON - nearest) * math.log(root))) * factor
    table = np.zeros((LANES, LANES), np.float32)
    table[:LON, :LON] = values
    return table.astype(BF)


def row_factors():
    rows = np.arange(-HALO, TOTAL_ROWS + HALO)
    cosine = np.cos(math.pi * ((rows + 0.5) / TOTAL_ROWS - 0.5))
    metric = 1.0 / (cosine * cosine + 0.1)
    inside = (rows >= 0) & (rows < TOTAL_ROWS)
    return np.stack([metric / (2 + 2 * metric), 1 / (2 + 2 * metric), inside], axis=1).astype(np.float32)


def hot(condition):
    return jnp.where(condition, 1.0, 0.0).astype(BF)


def iota(shape, dim):
    return lax.broadcasted_iota(jnp.int32, shape, dim)


def grid_to_message(transposed):
    shape = (320, 256) if transposed else (256, 320)
    row, col = iota(shape, int(transposed)), iota(shape, 1 - int(transposed))
    group, place = row >> 4, row & 15
    main = hot(col == (place >> 2) * FIELDS + group * 5 + (place & 3))
    fifth = col == (place & 3) * FIELDS + group * 5 + 4
    return main, [hot(fifth & ((place >> 2) == t)) for t in range(TILES)]


def message_to_station(transposed):
    shape = (256, 512) if transposed else (512, 256)
    row, col = iota(shape, int(transposed)), iota(shape, 1 - int(transposed))
    r, member, f = row >> 7, (row >> 3) & 15, row & 7
    same = member == (col >> 4)
    place = col & 15
    main = hot(same & (f < 4) & (place == r * 4 + f))
    return main, [hot(same & (f == 4) & (place == t * 4 + r)) for t in range(TILES)]


def lane_tile(t):
    return slice(t * 128, (t + 1) * 128)


def lane_chunk(q):
    return slice(q * CHUNK, (q + 1) * CHUNK)


def dot(a, b):
    return jnp.dot(a, b, preferred_element_type=F32)


def dot_t(a, b):
    return lax.dot_general(a, b, (((1,), (1,)), ((), ())), preferred_element_type=F32)


def stencil_row(u, nxt, weight, row, east_west, north_south, inside):
    tiles = LANES // 128
    lane = iota((FIELDS, 128), 1)

    def tile(at, t):
        return u[at, :, t * 128 : (t + 1) * 128].astype(F32)

    first, last = tile(row, 0), tile(row, tiles - 1)
    wrapped = jnp.where(lane == LON % 128, pltpu.roll(first, LON % 128, 1), last)
    before = pltpu.roll(last, 129 - LON % 128, 1)
    here = first
    ahead = pltpu.roll(here, 127, 1)
    for pair in range(tiles // 2):
        values, middles = [], []
        for t in (2 * pair, 2 * pair + 1):
            after = wrapped if t == tiles - 2 else (tile(row, t + 1) if t < tiles - 1 else here)
            further = pltpu.roll(after, 127, 1) if t < tiles - 1 else ahead
            east = jnp.where(lane == 127, further, ahead)
            moved = pltpu.roll(here, 1, 1)
            west = jnp.where(lane == 0, before, moved)
            sides = tile(row - 1, t) + tile(row + 1, t)
            values.append((east + west) * east_west + sides * north_south - here)
            middles.append(here)
            before, here, ahead = moved, after, further
        mixed = dot(weight, jnp.concatenate(values, axis=1).astype(BF))
        fresh = jnp.concatenate(middles, axis=1) + jnp.tanh(mixed)
        if inside is not None:
            fresh = fresh * inside
        nxt[row, :, pair * 256 : (pair + 1) * 256] = fresh.astype(BF)


def diffuse_chunk(q, rows, inverse, main, fifth, message):
    piece = dot(rows, inverse[:, lane_chunk(q)]).astype(BF)
    message[q, :, :, :CHUNK] = dot(main, piece).astype(BF).reshape(MEMBERS, 16, CHUNK)
    below = sum(dot(fifth[t], piece[:, lane_tile(t)]) for t in range(TILES))
    message[q, :, :, CHUNK:] = below.astype(BF).reshape(MEMBERS, 16, 128)


def pair_terms(values, truth):
    slopes = [None] * MEMBERS
    total = None
    for i in range(MEMBERS):
        for j in range(i + 1, MEMBERS):
            spread = values[i] - values[j]
            square = spread * spread + 1.0
            inverse = lax.rsqrt(square)
            slope = spread * inverse
            root = square * inverse
            total = root if total is None else total + root
            slopes[i] = slope if slopes[i] is None else slopes[i] + slope
            slopes[j] = -slope if slopes[j] is None else slopes[j] - slope
    error_total = None
    grads = []
    for m in range(MEMBERS):
        error = values[m] - truth
        square = error * error + 1.0
        inverse = lax.rsqrt(square)
        root = square * inverse
        error_total = root if error_total is None else error_total + root
        grads.append(error * inverse - slopes[m] * (1.0 / (MEMBERS - 1)))
    score = (error_total - MEMBERS) * (1.0 / MEMBERS) - (total - PAIRS) * (1.0 / (MEMBERS * (MEMBERS - 1)))
    return score, grads


def send(src, dst, sems, device):
    return pltpu.make_async_remote_copy(
        src_ref=src,
        dst_ref=dst,
        send_sem=sems.at[0],
        recv_sem=sems.at[1],
        device_id=device,
        device_id_type=pl.DeviceIdType.MESH,
    )


def member_at(member, step, sign):
    x = (member + sign * (step & 3)) & 3
    y = ((member >> 2) + sign * (step >> 2)) & 3
    return y * 4 + x


def band_at(band, step, sign):
    return (band + sign * step) & (BANDS - 1)


def exchange(source, target, sems, me, at, axis):
    @pl.loop(1, 16)
    def _(step):
        peer = at(me, step, 1)
        send(source(peer), target.at[me], sems, {axis: peer}).start()


def all_others(target, sems, me, at, axis):
    whole = target.at[0:15]
    return send(whole, whole, sems, {axis: at(me, 1, 1)})


def wait_received(source, target, sems, me, at, axis):
    all_others(target, sems, me, at, axis).wait_recv()


def wait_sent(source, target, sems, me, at, axis):
    all_others(target, sems, me, at, axis).wait_send()


def find_slots(band_ref, band, slot_ref):
    own = [band_ref[band * 16 + k] for k in range(16)]
    for k in range(16):
        rank = jnp.int32(0)
        for i in range(k):
            rank += jnp.where(own[i] == own[k], 1, 0)
        slot_ref[k] = own[k] * CAP + rank


def find_starts(band_ref, first_ref, band, start_ref):
    @pl.loop(0, BANDS)
    def _(home):
        seen, first, second = jnp.int32(0), jnp.int32(0), jnp.int32(0)
        for k in range(16):
            match = band_ref[home * 16 + k] == band
            here = first_ref[home * 16 + k]
            first = jnp.where(match & (seen == 0), here, first)
            second = jnp.where(match & (seen == 1), here, second)
            seen += jnp.where(match, 1, 0)
        start_ref[home * CAP] = first
        start_ref[home * CAP + 1] = second


def outgoing_shares(slot_ref, weight_ref, member, zout):
    row, col = iota((8, 128), 0), iota((8, 128), 1)
    own = hot(col == (16 + (member & 1) * 8 + row) * ROWS + ((member >> 1) & 3))
    share = jnp.concatenate([dot(own, weight_ref[k]) for k in range(16)], axis=0).astype(BF)
    lane = iota((1, 128), 1)
    slot_row = jnp.zeros((1, 128), jnp.int32)
    for k in range(16):
        slot_row = jnp.where((lane >> 3) == k, slot_ref[k], slot_row)
    row, col = iota((128, 128), 0), iota((128, 128), 1)
    pick = hot(((row >> 3) * CAP + (member >> 3) == slot_row) & ((row & 7) == (col & 7)))
    picked = dot(pick, share)
    for b in range(BANDS):
        zout[b] = jnp.concatenate([picked[b * 8 : b * 8 + 8], jnp.zeros((8, 128), F32)], axis=0).astype(BF)


def join_shares(zin, joined):
    for pair in range(BANDS // 2):
        parts = [zin[2 * pair + odd].astype(F32)[0:8] for odd in range(2)]
        joined[pair] = jnp.concatenate(parts, axis=0).astype(BF)


def outgoing_direct(slot_ref, weight_ref, turned, direct_out):
    row, col = iota((64, 128), 0), iota((64, 128), 1)
    pick = hot(col == (row & 15) * ROWS + (row >> 4))
    for k in range(16):
        turned[k] = dot(pick, weight_ref[k]).astype(BF)

    @pl.loop(0, BANDS)
    def _(b):
        for cap in range(CAP):
            block = jnp.zeros((64, 128), BF)
            for k in range(16):
                block = jnp.where(jnp.full((64, 128), slot_ref[k], jnp.int32) == b * CAP + cap, turned[k], block)
            direct_out[b, cap * 64 : (cap + 1) * 64, :] = block


def outgoing_obs(slot_ref, obs_ref, member, obs_out):
    row, col = iota((16, FIELDS), 0), iota((16, FIELDS), 1)
    pick = hot((row < 5) & (col == member * 5 + row))
    own = dot_t(pick, obs_ref[...].reshape(16 * STATIONS, FIELDS))[0:8]
    group = iota((8, 128), 1) >> 5
    blocks = []
    for k in range(16):
        block = jnp.where(group == (k & 3), own[:, lane_tile(k >> 2)], 0.0)
        block += pltpu.roll(block, 32, 1)
        blocks.append(block + pltpu.roll(block, 64, 1))
    for t in range(SLOTS // 4):
        tile = jnp.zeros((8, 128), F32)
        for k in range(16):
            tile = jnp.where(group + 4 * t == slot_ref[k], blocks[k], tile)
        for odd in range(2):
            piece = pltpu.roll(tile, 64, 1) if odd else tile
            obs_out[2 * t + odd] = jnp.concatenate([piece, jnp.zeros((8, 128), F32)], axis=0).astype(BF)


def spread_out_weights(start_ref, direct, weights, spread_weight):
    lane = iota((STATIONS, 128), 1)

    @pl.loop(0, BANDS // 2)
    def _(pair):
        for cap in range(CAP):
            shares = [
                [weights[cap * 8 + r * 2 + g, pair].astype(F32) for g in range(2)] for r in range(ROWS)
            ]
            for odd in range(2):
                home = pair * 2 + odd
                start = start_ref[home * CAP + cap]
                shift = start & 127
                at = pl.ds(home * 64 + cap * STATIONS, STATIONS)
                moved = []
                for r in range(ROWS):
                    near = direct[home, cap * 64 + r * 16 : cap * 64 + r * 16 + 16, :].astype(F32)
                    passed = [share[odd * 8 : odd * 8 + 8] for share in shares[r]]
                    moved.append(pltpu.roll(jnp.concatenate([near] + passed, axis=0), shift, 1))
                for t in range(LANES // 128):
                    place = lane + t * 128 - start
                    inside = (place >= 0) & (place < 128)
                    for r in range(ROWS):
                        spread_weight[r, at, lane_tile(t)] = jnp.where(inside, moved[r], 0.0).astype(BF)


def fold_truth(truth_ref, truth):
    truth[...] = jnp.zeros((CHUNKS, 16, PIECE), F32)
    fields = [truth_ref[f].astype(F32) for f in range(5)]
    for q in range(CHUNKS):
        width = min(CHUNK, LON - q * CHUNK)
        for r in range(ROWS):
            for f in range(4):
                truth[q, 4 * r + f : 4 * r + f + 1, :width] = fields[f][r : r + 1, q * CHUNK : q * CHUNK + width]
        for t in range(TILES):
            first = q * CHUNK + t * 128
            width = min(128, LON - first)
            truth[q, 4 * t : 4 * t + 4, CHUNK : CHUNK + width] = fields[4][:, first : first + width]


def unfold_score(score, score_ref):
    for q in range(CHUNKS):
        width = min(CHUNK, LON - q * CHUNK)
        for r in range(ROWS):
            for f in range(4):
                score_ref[f, r : r + 1, q * CHUNK : q * CHUNK + width] = score[
                    q, 4 * r + f : 4 * r + f + 1, :width
                ]
        for t in range(TILES):
            first = q * CHUNK + t * 128
            width = min(128, LON - first)
            score_ref[4, :, first : first + width] = score[q, 4 * t : 4 * t + 4, CHUNK : CHUNK + width]


def join_obs(obs_in, obs):
    lane = iota((8, 128), 1)
    for t in range(POINTS // 128):
        low = obs_in[2 * t].astype(F32)[0:8]
        high = obs_in[2 * t + 1].astype(F32)[0:8]
        obs[:, lane_tile(t)] = jnp.where(lane < 64, low, pltpu.roll(high, 64, 1))


def station_rows(q, received, main, fifth, rows):
    for t in range(TILES):
        tile = dot(main, received[q, :, :, lane_tile(t)].reshape(256, 128))
        tile += dot(fifth[t], received[q, :, :, CHUNK:].reshape(256, 128))
        rows[:, lane_tile(q * TILES + t)] = tile.astype(BF)


def estimates(first, stop, rows, spread_weight, est):
    for r in range(ROWS):
        part = dot_t(rows[r * 128 : (r + 1) * 128, first:stop], spread_weight[r, :, first:stop])
        est[...] = part if r == 0 and first == 0 else est[...] + part


def station_scores(est, slopes, obs, station_out):
    lane = iota((8, 128), 1)

    @pl.loop(0, POINTS // 256)
    def _(n):
        for half in range(2):
            at = pl.ds(pl.multiple_of(n * 256 + half * 128, 128), 128)
            members = [est[m * 8 : (m + 1) * 8, at] for m in range(MEMBERS)]
            total, grads = pair_terms(members, obs[:, at])
            other = pltpu.roll(total, 64, 1)
            station_out[4 * n + 2 * half] = jnp.where(lane < 64, total, other)
            station_out[4 * n + 2 * half + 1] = jnp.where(lane < 64, other, total)
            for m in range(0, MEMBERS, 2):
                slopes[m * 8 : m * 8 + 16, at] = jnp.concatenate(grads[m : m + 2], axis=0).astype(BF)


def grid_pairs(q, received, values, truth, score):
    values[q] = received[q].astype(F32)

    @pl.loop(0, PIECE // 128)
    def _(n):
        at = pl.ds(pl.multiple_of(n * 128, 128), 128)
        for half in range(2):
            part = slice(half * 8, half * 8 + 8)
            members = [values[q, m, part, at] for m in range(MEMBERS)]
            total, grads = pair_terms(members, truth[q, part, at])
            score[q, part, at] = total
            for m in range(MEMBERS):
                values[q, m, part, at] = grads[m]


def spread_chunk(q, slopes, spread_weight, spread):
    for r in range(ROWS):
        part = dot(slopes[...], spread_weight[r, :, lane_chunk(q)])
        spread[r * 128 : (r + 1) * 128, :] = part.astype(BF)


def total_chunk(q, values, spread, back, back_fifth, grad):
    total = values[q, :, :, :CHUNK].reshape(256, CHUNK) + dot(back, spread[...])
    grad[q, :, :, :CHUNK] = total.astype(BF).reshape(MEMBERS, 16, CHUNK)
    below = values[q, :, :, CHUNK:].reshape(256, 128)
    for t in range(TILES):
        below += dot(back_fifth[t], spread[:, lane_tile(t)])
    grad[q, :, :, CHUNK:] = below.astype(BF).reshape(MEMBERS, 16, 128)


def own_station_scores(slot_ref, station_in, own):
    group = iota((8, 128), 1) >> 5
    even = (group & 1) == 0
    pieces = []
    for b in range(BANDS):
        here = station_in[b]
        moved = pltpu.roll(here, 32, 1)
        pieces.append(jnp.where(even, here, moved))
        pieces.append(jnp.where(even, moved, here))
    tiles = []
    for t in range(4):
        slot = jnp.zeros((8, 128), jnp.int32)
        for g in range(4):
            slot = jnp.where(group == g, slot_ref[4 * t + g], slot)
        tile = jnp.zeros((8, 128), F32)
        for at in range(SLOTS):
            tile = jnp.where(slot == at, pieces[at], tile)
        tiles.append(tile)
    for t in range(2):
        own[:, lane_tile(t)] = jnp.concatenate([tiles[t], tiles[t + 2]], axis=0).astype(BF)


def all_station_scores(gathered, station_ref):
    row, col = iota((256, FIELDS), 0), iota((256, FIELDS), 1)
    field = (row >> 4) * 5 + (row & 7)
    whole = gathered[...].reshape(256, 256)
    dims = (((0,), (0,)), ((), ()))
    for half in range(2):
        pick = hot(((row & 7) < 5) & (field == col) & (((row >> 3) & 1) == half))
        joined = lax.dot_general(whole, pick, dims, preferred_element_type=F32)
        station_ref[half * 8 : half * 8 + 8] = joined.reshape(8, STATIONS, FIELDS)


def add_state(q, returned, main, fifth, inverse, total, state, out, copies):
    for t in range(TILES):
        tile = dot(main, returned[q, :, :, lane_tile(t)].reshape(256, 128))
        tile += dot(fifth[t], returned[q, :, :, CHUNK:].reshape(256, 128))
        total[:, lane_tile(t)] = tile.astype(BF)
    for n in range(CHUNKS):
        width = min(CHUNK, LON - n * CHUNK)
        at = slice(n * CHUNK, n * CHUNK + width)
        part = dot(total[...], inverse[lane_chunk(q), at])
        if q > 0:
            part += state[:, at]
        if q < CHUNKS - 1:
            state[:, at] = part
        else:
            out[0, :, :, at] = part.astype(BF).reshape(ROWS, FIELDS, width)
            copies[n].start()


def kernel(
    band_ref, first_ref, factor_ref, state_hbm, mix_ref, weight_hbm, obs_hbm, truth_hbm, inverse_hbm,
    score_ref, station_ref, out_ref,
    start_ref, slot_ref,
    state_ref, weight_ref, obs_ref, truth_ref,
    layers, inverse, zout, zin, joined, turned, direct_out, direct_in, obs_out, obs_in, weights, spread_weight, message, received, grad, returned,
    rows, est, slopes, values, spread, truth, obs, score, station_out, station_in, own, gathered,
    total, state, score_out, scores_out, out,
    fetch_sem, leave_sem, halo_sem, z_sem, obs_sem, direct_sem, weight_sem, message_sem, station_sem, own_sem, grad_sem,
):
    band = lax.axis_index("band")
    member = lax.axis_index("member")
    barrier = pltpu.get_barrier_semaphore()

    @pl.loop(1, 16)
    def _(step):
        for device in ({"member": member_at(member, step, 1)}, {"band": band_at(band, step, 1)}):
            pl.semaphore_signal(barrier, inc=1, device_id=device, device_id_type=pl.DeviceIdType.MESH)

    fetches = [
        pltpu.make_async_copy(source, target, fetch_sem.at[i])
        for i, (source, target) in enumerate(
            [(state_hbm.at[0, r], state_ref.at[0, r]) for r in range(ROWS)]
            + [
                (weight_hbm, weight_ref), (obs_hbm, obs_ref), (truth_hbm, truth_ref),
                (inverse_hbm, inverse),
            ]
        )
    ]
    for fetch in fetches:
        fetch.start()

    u = layers.at[0]
    u[HALO : HALO + ROWS, :, LON - 32 :] = jnp.zeros((ROWS, FIELDS, LANES - LON + 32), BF)

    @pl.when(band == 0)
    def _():
        u[0:HALO] = jnp.zeros((HALO, FIELDS, LANES), BF)

    @pl.when(band == BANDS - 1)
    def _():
        u[HALO + ROWS :] = jnp.zeros((HALO, FIELDS, LANES), BF)

    find_slots(band_ref, band, slot_ref)
    for fetch in fetches[:ROWS]:
        fetch.wait()
    u[HALO : HALO + ROWS, :, :LON] = state_ref[0]

    def to_north(i):
        return send(u.at[HALO + ROWS - 1 - i], u.at[HALO - 1 - i], halo_sem.at[i], {"band": band_at(band, 1, 1)})

    def to_south(i):
        return send(u.at[HALO + i], u.at[HALO + ROWS + i], halo_sem.at[HALO + i], {"band": band_at(band, 1, -1)})

    def send_halo(i):
        pl.when(band < BANDS - 1)(to_north(i).start)
        pl.when(band > 0)(to_south(i).start)

    direct_args = (lambda b: direct_out.at[b], direct_in, direct_sem, band, band_at, "band")
    weight_args = (lambda m: joined, weights, weight_sem, member, member_at, "member")
    z_args = (lambda b: zout.at[b], zin, z_sem, band, band_at, "band")
    obs_args = (lambda b: obs_out.at[b], obs_in, obs_sem, band, band_at, "band")
    station_args = (lambda b: station_out.at[b], station_in, station_sem, band, band_at, "band")
    own_args = (lambda m: own, gathered, own_sem, member, member_at, "member")

    def message_args(q):
        return lambda m: message.at[q, m], received.at[q], message_sem.at[q], member, member_at, "member"

    def grad_args(q):
        return lambda m: grad.at[q, m], returned.at[q], grad_sem.at[q], member, member_at, "member"

    def run_pair(layer, low, high):
        own = HALO <= low and high < HALO + ROWS
        for row in (low, high):
            factor = band * ROWS + row
            stencil_row(
                layers.at[layer], layers.at[layer + 1], mix_ref[layer], row,
                factor_ref[factor, 0], factor_ref[factor, 1], None if own else factor_ref[factor, 2],
            )

    def wait_halo(i):
        pl.when(band > 0)(to_north(i).wait_recv)
        pl.when(band < BANDS - 1)(to_south(i).wait_recv)

    run_pair(0, 4, 5)
    fetches[ROWS].wait()
    outgoing_shares(slot_ref, weight_ref, member, zout)
    fetches[ROWS + 1].wait()
    outgoing_obs(slot_ref, obs_ref, member, obs_out)
    outgoing_direct(slot_ref, weight_ref, turned, direct_out)
    pl.semaphore_wait(barrier, 30)
    send_halo(0)
    exchange(*z_args)
    send_halo(1)
    send_halo(2)
    zin[band] = zout[band]
    obs_in[band] = obs_out[band]
    direct_in[band] = direct_out[band]
    find_starts(band_ref, first_ref, band, start_ref)
    fetches[ROWS + 2].wait()
    fold_truth(truth_ref, truth)
    wait_halo(0)
    run_pair(0, 3, 6)
    run_pair(1, 4, 5)
    wait_received(*z_args)
    join_shares(zin, joined)
    exchange(*weight_args)
    weights[member] = joined[...]
    wait_halo(1)
    run_pair(0, 2, 7)
    exchange(*obs_args)
    exchange(*direct_args)
    run_pair(1, 3, 6)
    run_pair(2, 4, 5)
    wait_halo(2)
    run_pair(0, 1, 8)
    run_pair(1, 2, 7)
    run_pair(2, 3, 6)

    fetches[ROWS + 3].wait()
    main, fifth = grid_to_message(False)
    grid_rows = layers[LAYERS, HALO : HALO + ROWS].reshape(ROWS * FIELDS, LANES)
    for q in range(CHUNKS):
        diffuse_chunk(q, grid_rows, inverse, main, fifth, message)
        exchange(*message_args(q))
        received[q, member] = message[q, member]

    main, fifth = message_to_station(False)
    for q in range(CHUNKS - 1):
        wait_received(*message_args(q))
        station_rows(q, received, main, fifth, rows)
        grid_pairs(q, received, values, truth, score)
        if q == CHUNKS - 2:
            wait_received(*obs_args)
            join_obs(obs_in, obs)
            wait_received(*weight_args)
            wait_received(*direct_args)
            spread_out_weights(start_ref, direct_in, weights, spread_weight)

    estimates(0, CHUNK * (CHUNKS - 1), rows, spread_weight, est)
    wait_received(*message_args(CHUNKS - 1))
    station_rows(CHUNKS - 1, received, main, fifth, rows)
    estimates(CHUNK * (CHUNKS - 1), LANES, rows, spread_weight, est)
    station_scores(est, slopes, obs, station_out)
    def share_station_scores():
        wait_received(*station_args)
        own_station_scores(slot_ref, station_in, own)
        exchange(*own_args)
        gathered[member] = own[...]

    back, back_fifth = message_to_station(True)
    for q in range(CHUNKS):
        spread_chunk(q, slopes, spread_weight, spread)
        if q == CHUNKS - 1:
            grid_pairs(q, received, values, truth, score)
        total_chunk(q, values, spread, back, back_fifth, grad)
        exchange(*grad_args(q))
        if q == 0:
            exchange(*station_args)
            station_in[band] = station_out[band]
        returned[q, member] = grad[q, member]

    leave = [
        pltpu.make_async_copy(score_out, score_ref, leave_sem.at[0]),
        pltpu.make_async_copy(scores_out, station_ref, leave_sem.at[1]),
    ]
    leave_state = []
    for n in range(CHUNKS):
        at = slice(n * CHUNK, min((n + 1) * CHUNK, LON))
        leave_state.append(pltpu.make_async_copy(out.at[:, :, :, at], out_ref.at[:, :, :, at], leave_sem.at[2 + n]))
    unfold_score(score, score_out)
    leave[0].start()
    share_station_scores()
    for i in range(HALO):
        pl.when(band < BANDS - 1)(to_north(i).wait_send)
        pl.when(band > 0)(to_south(i).wait_send)
    for args in (obs_args, z_args, direct_args, weight_args, station_args):
        wait_sent(*args)
    for q in range(CHUNKS):
        wait_sent(*message_args(q))

    main, fifth = grid_to_message(True)
    for q in range(CHUNKS):
        wait_received(*grad_args(q))
        add_state(q, returned, main, fifth, inverse, total, state, out, leave_state)
        wait_sent(*grad_args(q))
    wait_received(*own_args)
    all_station_scores(gathered, scores_out)
    leave[1].start()
    wait_sent(*own_args)
    for copy in leave:
        copy.wait()
    for copy in leave_state:
        copy.wait()


def hand_over(*refs):
    count = len(refs) // 2
    for i in range(count):
        refs[count + i][...] = refs[i][...]


def shards(ensemble, mix_weight, analysis, station_weight, station_obs, block_band, block_start):
    smem = pl.BlockSpec(memory_space=pltpu.SMEM)
    vmem = pl.BlockSpec(memory_space=pltpu.VMEM)
    anywhere = pl.BlockSpec(memory_space=pl.ANY)
    message = (CHUNKS, MEMBERS, 16, PIECE)
    sems = pltpu.SemaphoreType.DMA((2,))
    piece_sems = pltpu.SemaphoreType.DMA((CHUNKS, 2))
    shapes = (
        jax.ShapeDtypeStruct((5, ROWS, LON), F32),
        jax.ShapeDtypeStruct((16, STATIONS, FIELDS), F32),
        jax.ShapeDtypeStruct((1, ROWS, FIELDS, LON), BF),
    )
    outs = pl.pallas_call(
        kernel,
        out_shape=tuple(pltpu.VMEM(shape.shape, shape.dtype) for shape in shapes),
        in_specs=[smem] * 3 + [anywhere, vmem] + [anywhere] * 4,
        out_specs=(anywhere,) * 3,
        scratch_shapes=[
            pltpu.SMEM((SLOTS,), jnp.int32),
            pltpu.SMEM((16,), jnp.int32),
            pltpu.VMEM((1, ROWS, FIELDS, LON), BF),
            pltpu.VMEM((16, STATIONS * ROWS, 128), BF),
            pltpu.VMEM((16, STATIONS, FIELDS), BF),
            pltpu.VMEM((5, ROWS, LON), BF),
            pltpu.VMEM((LAYERS + 1, EXT, FIELDS, LANES), BF),
            pltpu.VMEM((LANES, LANES), BF),
            pltpu.VMEM((BANDS, 16, 128), BF),
            pltpu.VMEM((BANDS, 16, 128), BF),
            pltpu.VMEM((BANDS // 2, 16, 128), BF),
            pltpu.VMEM((16, 64, 128), BF),
            pltpu.VMEM((BANDS, 128, 128), BF),
            pltpu.VMEM((BANDS, 128, 128), BF),
            pltpu.VMEM((BANDS, 16, 128), BF),
            pltpu.VMEM((BANDS, 16, 128), BF),
            pltpu.VMEM((MEMBERS, BANDS // 2, 16, 128), BF),
            pltpu.VMEM((ROWS, POINTS, LANES), BF),
            pltpu.VMEM(message, BF),
            pltpu.VMEM(message, BF),
            pltpu.VMEM(message, BF),
            pltpu.VMEM(message, BF),
            pltpu.VMEM((512, LANES), BF),
            pltpu.VMEM((128, POINTS), F32),
            pltpu.VMEM((128, POINTS), BF),
            pltpu.VMEM(message, F32),
            pltpu.VMEM((512, CHUNK), BF),
            pltpu.VMEM((CHUNKS, 16, PIECE), F32),
            pltpu.VMEM((8, POINTS), F32),
            pltpu.VMEM((CHUNKS, 16, PIECE), F32),
            pltpu.VMEM((BANDS, 8, 128), F32),
            pltpu.VMEM((BANDS, 8, 128), F32),
            pltpu.VMEM((16, 256), BF),
            pltpu.VMEM((MEMBERS, 16, 256), BF),
            pltpu.VMEM((ROWS * FIELDS, CHUNK), BF),
            pltpu.VMEM((ROWS * FIELDS, LON), F32),
            pltpu.VMEM((5, ROWS, LON), F32),
            pltpu.VMEM((16, STATIONS, FIELDS), F32),
            pltpu.VMEM((1, ROWS, FIELDS, LON), BF),
            pltpu.SemaphoreType.DMA((ROWS + 4,)),
            pltpu.SemaphoreType.DMA((2 + CHUNKS,)),
            pltpu.SemaphoreType.DMA((2 * HALO, 2)),
            sems, sems, sems, sems, piece_sems, sems, sems, piece_sems,
        ],
        compiler_params=pltpu.CompilerParams(
            vmem_limit_bytes=56 * MIB, collective_id=0, has_side_effects=True
        ),
    )(
        block_band.reshape(-1), block_start, jnp.asarray(row_factors()), ensemble, mix_weight,
        station_weight.reshape(16, STATIONS * ROWS, 128),        station_obs, jnp.transpose(analysis, (1, 0, 2)), jnp.asarray(inverse_table()),
    )
    score, station, state = pl.pallas_call(
        hand_over,
        out_shape=shapes,
        in_specs=[vmem] * 3,
        out_specs=(vmem,) * 3,
        compiler_params=pltpu.CompilerParams(vmem_limit_bytes=16 * MIB),
    )(*outs)
    return jnp.transpose(score, (1, 0, 2)), station, state


def solution(mesh):
    return jax.shard_map(
        shards,
        mesh=mesh,
        in_specs=(
            P("member", "band", None, None),
            P(),
            P("band", "member", None),
            P("band", None, None, None),
            P("band", None, None),
            P(),
            P(),
        ),
        out_specs=(
            P("band", "member", None),
            P("band", None, None),
            P("member", "band", None, None),
        ),
        check_vma=False,
    )
```
